256 devices in a mesh: row: 8 (over x, y_hi), col: 32 (over z, y_lo, core).
Axes of the slice: x: 4, y: 4 (y_hi: 2, y_lo: 2; y = y_hi * 2 + y_lo), z: 8, core: 2. Of those that a mesh axis runs over, the one named last changes fastest.
Arguments:
- node_features: float32 [32768, 256], P(('col', 'row')), may hold values from -6 to 6
- weight: float32 [256, 256], replicated, may hold values from -0.375 to 0.375
- bias: float32 [256], replicated, may hold values from -3 to 3
- tile_values: float32 [8, 32, 12, 128, 128], P('row', 'col'), may hold values from -0.25 to 0.25
- tile_coords: int32 [8, 32, 12, 2], P('row', 'col'), may hold values from 0 to 31, as said below
- tile_count: int32 [8, 32], P('row', 'col'), may hold values from 1 to 12, as said below
- cotangent: float32 [32768, 256], P(('row', 'col')), may hold values from -6 to 6
Outputs:
- output: float32 [32768, 256], P(('row', 'col'))
- input_grad: float32 [32768, 256], P(('col', 'row'))
- weight_grad: float32 [256, 256], replicated
- bias_grad: float32 [256], replicated
The draws below stay inside these ranges and needn't reach their ends.
Inputs may be any that keep to these rules, and one draw needn't show every extreme that they name: tile_coords[..., 0] is a tile row within the block row of 4096 nodes, tile_coords[..., 1] a tile column within the block column of 1024 nodes, each below that block's number of tiles; a position may stand in several slots, whose blocks add. Slots 0 to tile_count - 1 of a device are live; some device has all 12 live.
All inputs are finite; a program needn't handle non-finite values.
Results may differ from the reference program's by a relative error of at most 0.0003.
Values sent between devices are 32-bit elements; how exact they have to be, the bound alone decides.
No kernel may reach another device: no remote copies, remote signals or barrier semaphores. Data moves between devices by JAX's collectives and lax.ppermute only.
A program may use at most 64 MiB of HBM per device.

```python
import math
import jax
import jax.numpy as jnp
from jax import lax

F = 256
TILE = 128
ND = 128
CAP = 12
NODES = 32768
N_ROW = 8
N_COL = 32


def draw_tile_coords(key, part):
    key = jax.random.fold_in(key, 11)
    row_key, col_key = jax.random.split(key)
    tile_rows = jax.random.randint(row_key, (N_ROW, N_COL, CAP, 1), 0, ND * N_COL // TILE, dtype=jnp.int32)
    tile_cols = jax.random.randint(col_key, (N_ROW, N_COL, CAP, 1), 0, ND * N_ROW // TILE, dtype=jnp.int32)
    return jnp.concatenate([tile_rows, tile_cols], axis=3)


def draw_tile_count(key, part):
    key = jax.random.fold_in(key, 23)
    first_key, second_key = jax.random.split(key)
    base_draw = jax.random.randint(first_key, (N_ROW * N_COL,), 1, CAP + 1, dtype=jnp.int32)
    skewed = jnp.maximum(base_draw * base_draw // CAP, 1)
    heavy_device = jax.random.randint(second_key, (), 0, N_ROW * N_COL, dtype=jnp.int32)
    flattened = jnp.where(jnp.arange(N_ROW * N_COL, dtype=jnp.int32) == heavy_device, CAP, skewed)
    return flattened.reshape(N_ROW, N_COL).astype(jnp.int32)


def shard_levels(own_key, shape, cuts, low, top_value):
    loudness = 1.0
    for dim, blocks in cuts:
        steps = jax.random.uniform(jax.random.fold_in(jax.random.fold_in(own_key, 6), dim), (blocks,), jnp.float32, low / len(cuts), top_value / len(cuts))
        loudness = loudness * jnp.repeat(jnp.exp(steps), shape[dim] // blocks).reshape((-1,) + (1,) * (len(shape) - 1 - dim))
    return loudness


def noise(own_key, shape, width, limit, cuts=(), kind=jnp.bfloat16):
    level = shard_levels(own_key, shape, cuts, -0.22, 0.18) if cuts else 1.0
    entries = jax.random.normal(own_key, shape, jnp.float32) * width * level
    return jnp.minimum(jnp.maximum(entries, -limit), limit).astype(kind)


def setup_inputs(seed: int = 0) -> dict:
    arg_keys = jax.random.split(jax.random.key(seed), 8)
    return {
        "node_features": noise(arg_keys[0], (NODES, F), 1.0, 6.0, ((0, 256),), jnp.float32),
        "weight": noise(arg_keys[1], (F, F), F ** -0.5, 0.375, (), jnp.float32),
        "bias": noise(arg_keys[2], (F,), 0.5, 3.0, (), jnp.float32),
        "tile_values": noise(arg_keys[3], (N_ROW, N_COL, CAP, TILE, TILE), (CAP * TILE * TILE // (3 * ND)) ** -0.5, 0.25, ((0, 8), (1, 32)), jnp.float32),
        "tile_coords": draw_tile_coords(jax.random.fold_in(arg_keys[7], 71), 0),
        "tile_count": draw_tile_count(jax.random.fold_in(arg_keys[7], 71), 0),
        "cotangent": noise(arg_keys[6], (NODES, F), 1.0, 6.0, ((0, 256),), jnp.float32),
    }


def aggregate(tile_values, tile_coords, tile_count, features, transpose):
    row_tiles = ND * N_COL // TILE
    col_tiles = ND * N_ROW // TILE
    blocks = features.reshape(NODES // TILE, TILE, F)
    device_count = N_ROW * N_COL
    flat_values = tile_values.reshape(device_count, CAP, TILE, TILE)
    flat_coords = tile_coords.reshape(device_count, CAP, 2)
    flat_count = tile_count.reshape(device_count)
    device_ids = jnp.arange(device_count, dtype=jnp.int32)

    def step(total, inputs):
        values, positions, live_count, device = inputs
        row_block = device // N_COL
        col_block = device % N_COL
        global_rows = (row_block * row_tiles + positions[:, 0]).astype(jnp.int32)
        global_cols = (col_block * col_tiles + positions[:, 1]).astype(jnp.int32)
        live_mask = (jnp.arange(CAP, dtype=jnp.int32) < live_count).astype(total.dtype)[:, None, None]
        if transpose:
            picked = blocks[global_cols * 0 + global_rows]
            products = jnp.einsum('kji,kjf->kif', values, picked, precision=lax.Precision.HIGHEST)
            target = global_cols
        else:
            picked = blocks[global_cols]
            products = jnp.einsum('kij,kjf->kif', values, picked, precision=lax.Precision.HIGHEST)
            target = global_rows
        return (total.at[target].add(products * live_mask), None)
    start = jnp.zeros((NODES // TILE, TILE, F), features.dtype)
    total, unused = lax.scan(step, start, (flat_values, flat_coords, flat_count, device_ids))
    return total.reshape(NODES, F)

def reference(node_features, weight, bias, tile_values, tile_coords, tile_count, cotangent):
    precise = lax.Precision.HIGHEST
    transformed = jnp.dot(node_features, weight, precision=precise)
    aggregated = aggregate(tile_values, tile_coords, tile_count, transformed, False)
    pre = aggregated + bias
    sigma = jax.nn.sigmoid(pre)
    output = pre * sigma
    pre_grad = cotangent * (sigma * (1.0 + pre * (1.0 - sigma)))
    back = aggregate(tile_values, tile_coords, tile_count, pre_grad, True)
    input_grad = jnp.dot(back, weight.T, precision=precise)
    factor = 1.0 / math.sqrt(NODES)
    weight_grad = jnp.dot(node_features.T, back, precision=precise) * factor
    bias_grad = lax.optimization_barrier(jnp.sum(pre_grad, axis=0)) * factor
    return (output, input_grad, weight_grad, bias_grad)
```

```python
import math

import jax
import jax.numpy as jnp
from jax import lax
from jax.experimental import pallas as pl
from jax.experimental.pallas import tpu as pltpu
from jax.sharding import PartitionSpec as P

Z, YL = 8, 2
TILE = 128


def col_pairs(move):
    pairs = []
    for z in range(Z):
        for y in range(YL):
            for core in range(2):
                a, b, c = move(z, y, core)
                pairs.append(((z * YL + y) * 2 + core, (a * YL + b) * 2 + c))
    return pairs


CORE_SWAP = col_pairs(lambda z, y, core: (z, y, 1 - core))
Y_SWAP = col_pairs(lambda z, y, core: (z, 1 - y, core))
Z_GROUPS = [[(z * YL + y) * 2 + core for z in range(Z)] for y in range(YL) for core in range(2)]


def split(value):
    high = value.astype(jnp.bfloat16)
    low = (value - high.astype(jnp.float32)).astype(jnp.bfloat16)
    return high, low


def dot3(left, right, contract):
    def one(a, b):
        return lax.dot_general(a, b, (contract, ((), ())), preferred_element_type=jnp.float32)

    return one(left[0], right[0]) + (one(left[0], right[1]) + one(left[1], right[0]))


def forward_kernel(place, count, core, values, features, keep, send, total, high, low, sems):
    total[...] = jnp.zeros_like(total)
    for j in range(features.shape[0]):
        high[j], low[j] = split(features[j])

    def slot(k, carry):
        row, col = place[k, 0], place[k, 1]
        parity = lax.rem(row, 2)
        half = jnp.where(parity == core[0], 0, 1)
        product = dot3(split(values[k]), (high[col], low[col]), ((1,), (0,)))
        index = half * keep.shape[0] + lax.div(row, 2)
        total[index] += product
        return carry

    lax.fori_loop(0, count[0], slot, 0)
    tiles = keep.shape[0]
    copies = [
        pltpu.make_async_copy(total.at[pl.ds(tiles, tiles)], send, sems.at[0]),
        pltpu.make_async_copy(total.at[pl.ds(0, tiles)], keep, sems.at[1]),
    ]
    for copy in copies:
        copy.start()
    for copy in copies:
        copy.wait()


def forward(place, count, core, values, features):
    tiles = Z * YL
    width = features.shape[-1]
    shape = jax.ShapeDtypeStruct((tiles, TILE, width), jnp.float32)
    smem = pl.BlockSpec(memory_space=pltpu.SMEM)
    vmem = pl.BlockSpec(memory_space=pltpu.VMEM)
    return pl.pallas_call(
        forward_kernel,
        out_shape=(shape, shape),
        in_specs=[smem, smem, smem, vmem, vmem],
        out_specs=(pl.BlockSpec(memory_space=pl.ANY),) * 2,
        scratch_shapes=[
            pltpu.VMEM((2 * tiles, TILE, width), jnp.float32),
            pltpu.VMEM(features.shape, jnp.bfloat16),
            pltpu.VMEM(features.shape, jnp.bfloat16),
            pltpu.SemaphoreType.DMA((2,)),
        ],
        compiler_params=pltpu.CompilerParams(vmem_limit_bytes=24 * 1024 * 1024),
        name="forward_tiles",
    )(place, count, core, values, features)


def middle_kernel(y_ref, mine, other, weight, bias, cot_own, cot_other, output, grad, extra, summed):
    y = y_ref[0]
    summed[...] = mine[...] + other[...]
    weights = split(weight[...])

    def half(start, cot):
        rows = pl.ds(pl.multiple_of(start, TILE), TILE)
        part = split(summed[rows, :])
        pre = dot3(part, weights, ((1,), (0,))) + bias[...]
        sigma = jax.nn.sigmoid(pre)
        value = cot[...] * (sigma * (1.0 + pre * (1.0 - sigma)))
        grad[rows, :] = value
        return part, pre * sigma, value

    half((1 - y) * TILE, cot_other)
    part, result, value = half(y * TILE, cot_own)
    output[...] = result
    value = split(value)
    width = weight.shape[1]
    extra[:, :width] = dot3(part, value, ((0,), (0,)))
    ones = jnp.ones((TILE, 128), jnp.bfloat16)
    first = lax.dot_general(value[0], ones, (((0,), (0,)), ((), ())), preferred_element_type=jnp.float32)
    second = lax.dot_general(value[1], ones, (((0,), (0,)), ((), ())), preferred_element_type=jnp.float32)
    extra[:, width:] = first + second


def middle(y, mine, other, weight, bias, cot_own, cot_other):
    width = weight.shape[1]
    smem = pl.BlockSpec(memory_space=pltpu.SMEM)
    vmem = pl.BlockSpec(memory_space=pltpu.VMEM)
    return pl.pallas_call(
        middle_kernel,
        out_shape=(
            jax.ShapeDtypeStruct((TILE, width), jnp.float32),
            jax.ShapeDtypeStruct((YL * TILE, width), jnp.float32),
            jax.ShapeDtypeStruct((weight.shape[0], width + 128), jnp.float32),
        ),
        in_specs=[smem] + [vmem] * 6,
        out_specs=(vmem,) * 3,
        scratch_shapes=[pltpu.VMEM((YL * TILE, weight.shape[0]), jnp.float32)],
        compiler_params=pltpu.CompilerParams(vmem_limit_bytes=16 * 1024 * 1024),
        name="middle",
    )(y, mine, other, weight, bias, cot_own, cot_other)


def backward_kernel(place, count, core, values, own, other, back):
    back[...] = jnp.zeros_like(back)

    def slot(k, carry):
        row, col = place[k, 0], place[k, 1]
        index = lax.div(row, 2)
        mine = lax.rem(row, 2) == core[0]
        block = jnp.where(mine, own[index], other[index])
        back[col] += dot3(split(values[k]), split(block), ((0,), (0,)))
        return carry

    lax.fori_loop(0, count[0], slot, 0)


def backward(place, count, core, values, own, other, tiles):
    smem = pl.BlockSpec(memory_space=pltpu.SMEM)
    vmem = pl.BlockSpec(memory_space=pltpu.VMEM)
    return pl.pallas_call(
        backward_kernel,
        out_shape=jax.ShapeDtypeStruct((tiles,) + own.shape[1:], jnp.float32),
        in_specs=[smem, smem, smem, vmem, vmem, vmem],
        out_specs=vmem,
        compiler_params=pltpu.CompilerParams(vmem_limit_bytes=24 * 1024 * 1024),
        name="backward_tiles",
    )(place, count, core, values, own, other)


def final_kernel(parts, weight, result):
    back = parts[0]
    for j in range(1, parts.shape[0]):
        back = back + parts[j]
    result[...] = dot3(split(back), split(weight[...]), ((1,), (1,)))


def final(parts, weight):
    vmem = pl.BlockSpec(memory_space=pltpu.VMEM)
    return pl.pallas_call(
        final_kernel,
        out_shape=jax.ShapeDtypeStruct((parts.shape[1], weight.shape[0]), jnp.float32),
        in_specs=[vmem, vmem],
        out_specs=vmem,
        compiler_params=pltpu.CompilerParams(vmem_limit_bytes=16 * 1024 * 1024),
        name="final",
    )(parts, weight)


def body(node_features, weight, bias, tile_values, tile_coords, tile_count, cotangent):
    values = tile_values[0, 0]
    place = tile_coords[0, 0]
    count = tile_count.reshape(1)
    local_nodes, width = node_features.shape
    row_count = lax.axis_size("row")
    col_count = lax.axis_size("col")
    device_count = row_count * col_count
    factor = 1.0 / math.sqrt(local_nodes * device_count)
    col = lax.axis_index("col")
    core = lax.rem(col, 2).reshape(1)
    y = lax.rem(lax.div(col, 2), YL).reshape(1)

    features = lax.all_to_all(
        jnp.broadcast_to(node_features[None], (row_count, local_nodes, width)), "row", 0, 0
    )
    keep, send = forward(place, count, core, values, features)
    partial = keep + lax.ppermute(send, "col", CORE_SWAP)
    summed = lax.psum_scatter(
        partial.reshape(Z * YL * TILE, width),
        "col",
        scatter_dimension=0,
        tiled=True,
        axis_index_groups=Z_GROUPS,
    )
    cot_other = lax.ppermute(cotangent, "col", Y_SWAP)
    summed, cot_other = lax.optimization_barrier((summed, cot_other))
    summed_other = lax.ppermute(summed, "col", Y_SWAP)
    output, grads, extra = middle(
        y, summed, summed_other, weight, bias.reshape(1, width), cotangent, cot_other
    )

    own = lax.all_gather(grads, "col", axis=0, tiled=True, axis_index_groups=Z_GROUPS)
    axes = ("row", "col")
    pieces = lax.all_to_all(extra.reshape(device_count, 1, -1), axes, 0, 0)
    piece = jnp.sum(pieces, axis=0, keepdims=True) * factor
    whole = lax.all_to_all(jnp.broadcast_to(piece, pieces.shape), axes, 0, 0)
    whole = whole.reshape(weight.shape[0], -1)
    weight_grad = whole[:, :width]
    bias_grad = whole[:, width]

    own, weight_grad, bias_grad = lax.optimization_barrier((own, weight_grad, bias_grad))
    own = own.reshape(Z * YL, TILE, width)
    other = lax.ppermute(own, "col", CORE_SWAP)
    back = backward(place, count, core, values, own, other, row_count)
    parts = lax.all_to_all(back, "row", 0, 0)
    input_grad = final(parts, weight)
    return (output, input_grad, weight_grad, bias_grad)


def solution(mesh):
    in_specs = (
        P(("col", "row"), None),
        P(),
        P(),
        P("row", "col", None, None, None),
        P("row", "col", None, None),
        P("row", "col"),
        P(("row", "col"), None),
    )
    out_specs = (P(("row", "col"), None), P(("col", "row"), None), P(), P())
    return jax.shard_map(body, mesh=mesh, in_specs=in_specs, out_specs=out_specs, check_vma=False)
```

```python
import math

import jax
import jax.numpy as jnp
from jax import lax
from jax.experimental import pallas as pl
from jax.experimental.pallas import tpu as pltpu
from jax.sharding import PartitionSpec as P

Z, YL = 8, 2
TILE = 128
PAIR = YL * TILE
NEAR = (0, 1, 2, 6, 7)
FAR = (3, 4, 5)


def col_pairs(move):
    pairs = []
    for z in range(Z):
        for y in range(YL):
            for core in range(2):
                a, b, c = move(z, y, core)
                pairs.append(((z * YL + y) * 2 + core, (a * YL + b) * 2 + c))
    return pairs


CORE_SWAP = col_pairs(lambda z, y, core: (z, y, 1 - core))
Y_SWAP = col_pairs(lambda z, y, core: (z, 1 - y, core))
Z_GROUPS = [[(z * YL + y) * 2 + core for z in range(Z)] for y in range(YL) for core in range(2)]


def z_shift(value, distance):
    return lax.ppermute(value, "col", col_pairs(lambda z, y, core: ((z + distance) % Z, y, core)))


SMEM = pl.BlockSpec(memory_space=pltpu.SMEM)
VMEM = pl.BlockSpec(memory_space=pltpu.VMEM)


def params(mib):
    return pltpu.CompilerParams(vmem_limit_bytes=mib * 1024 * 1024)


def shaped(*shape):
    return jax.ShapeDtypeStruct(shape, jnp.float32)


def split(value):
    high = value.astype(jnp.bfloat16)
    low = (value - high.astype(jnp.float32)).astype(jnp.bfloat16)
    return high, low


def dot3(left, right, contract):
    def one(a, b):
        return lax.dot_general(a, b, (contract, ((), ())), preferred_element_type=jnp.float32)

    return one(left[0], right[0]) + (one(left[0], right[1]) + one(left[1], right[0]))


def locate(tile, where):
    mine = lax.rem(tile, 2) == where[2]
    distance = lax.rem(lax.div(tile, 2 * YL) - where[0] + Z, Z)
    return mine, distance, lax.rem(lax.div(tile, 2), YL)


def forward_kernel(place, count, where, values, features, keep, send, total, high, low, sems):
    total[...] = jnp.zeros_like(total)
    for j in range(features.shape[0]):
        high[j], low[j] = split(features[j])

    def slot(k, carry):
        col = place[k, 1]
        mine, distance, y = locate(place[k, 0], where)
        product = dot3(split(values[k]), (high[col], low[col]), ((1,), (0,)))
        total[jnp.where(mine, 0, Z * YL) + distance * YL + y] += product
        return carry

    lax.fori_loop(0, count[0], slot, 0)
    tiles = keep.shape[0]
    copies = [
        pltpu.make_async_copy(total.at[pl.ds(tiles, tiles)], send, sems.at[0]),
        pltpu.make_async_copy(total.at[pl.ds(0, tiles)], keep, sems.at[1]),
    ]
    for copy in copies:
        copy.start()
    for copy in copies:
        copy.wait()


def forward(place, count, where, values, features):
    tiles = Z * YL
    width = features.shape[-1]
    return pl.pallas_call(
        forward_kernel,
        out_shape=(shaped(tiles, TILE, width),) * 2,
        in_specs=[SMEM, SMEM, SMEM, VMEM, VMEM],
        out_specs=(pl.BlockSpec(memory_space=pl.ANY),) * 2,
        scratch_shapes=[
            pltpu.VMEM((2 * tiles, TILE, width), jnp.float32),
            pltpu.VMEM(features.shape, jnp.bfloat16),
            pltpu.VMEM(features.shape, jnp.bfloat16),
            pltpu.SemaphoreType.DMA((2,)),
        ],
        compiler_params=params(24),
        name="forward_tiles",
    )(place, count, where, values, features)


def add_cores_kernel(first, second, own, one, two, three, four_up, four_down, five, six, seven):
    def total(tile):
        return first[tile] + second[tile]

    for distance, out in ((3, three), (5, five), (0, own), (1, one), (2, two), (6, six), (7, seven)):
        for y in range(YL):
            out[y * TILE : (y + 1) * TILE, :] = total(distance * YL + y)
    four_up[...] = total(4 * YL)
    four_down[...] = total(4 * YL + 1)


def add_cores(first, second):
    width = first.shape[-1]
    whole, half = shaped(PAIR, width), shaped(TILE, width)
    return pl.pallas_call(
        add_cores_kernel,
        out_shape=(whole,) * 4 + (half,) * 2 + (whole,) * 3,
        in_specs=[VMEM] * 2,
        out_specs=(VMEM,) * 9,
        compiler_params=params(16),
        name="add_cores",
    )(first, second)


def relay_kernel(two, three, four_up, six, five, four_down, up, down):
    up[:TILE, :] = two[:TILE, :] + three[:TILE, :] + four_up[...]
    up[TILE:, :] = two[TILE:, :] + three[TILE:, :]
    down[:TILE, :] = six[:TILE, :] + five[:TILE, :]
    down[TILE:, :] = six[TILE:, :] + five[TILE:, :] + four_down[...]


def relay(*operands):
    return pl.pallas_call(
        relay_kernel,
        out_shape=(jax.ShapeDtypeStruct(operands[0].shape, jnp.float32),) * 2,
        in_specs=[VMEM] * 6,
        out_specs=(VMEM,) * 2,
        compiler_params=params(16),
        name="relay",
    )(*operands)


def scatter_z(own, one, two, three, four_up, four_down, five, six, seven):
    from_three, from_five = z_shift(three, 1), z_shift(five, -1)
    from_up, from_down = z_shift(four_up, 2), z_shift(four_down, -2)
    from_one, from_seven = z_shift(one, 1), z_shift(seven, -1)
    up, down = relay(two, from_three, from_up, six, from_five, from_down)
    from_two, from_six = z_shift(up, 2), z_shift(down, -2)
    return ((own + from_one) + from_seven) + (from_two + from_six)


def middle_kernel(y_ref, mine, other, weight, bias, cot_own, cot_other, output, grad, extra, cots):
    y = y_ref[1]
    cots[y] = cot_own[...]
    cots[1 - y] = cot_other[...]
    cot = cots[...].reshape(grad.shape)
    part = split(mine[...] + other[...])
    pre = dot3(part, split(weight[...]), ((1,), (0,))) + bias[...]
    sigma = jax.nn.sigmoid(pre)
    value = cot * (sigma * (1.0 + pre * (1.0 - sigma)))
    grad[...] = value
    cots[...] = (pre * sigma).reshape(cots.shape)
    output[...] = cots[y]
    sums = jnp.broadcast_to(jnp.sum(value, axis=0, keepdims=True), (8, value.shape[1]))
    product = dot3(part, split(value), ((0,), (0,)))
    pieces = extra.shape[0]
    rows = product.shape[0] // pieces
    for j in range(pieces):
        extra[j, :rows, :] = product[j * rows : (j + 1) * rows, :]
        extra[j, rows:, :] = sums


def middle(where, mine, other, weight, bias, cot_own, cot_other, pieces):
    width = weight.shape[1]
    return pl.pallas_call(
        middle_kernel,
        out_shape=(
            shaped(TILE, width),
            shaped(PAIR, width),
            shaped(pieces, weight.shape[0] // pieces + 8, width),
        ),
        in_specs=[SMEM] + [VMEM] * 6,
        out_specs=(VMEM,) * 3,
        scratch_shapes=[pltpu.VMEM((YL, TILE, width), jnp.float32)],
        compiler_params=params(16),
        name="middle",
    )(where, mine, other, weight, bias, cot_own, cot_other)


def gather_z(block):
    one, seven = z_shift(block, -1), z_shift(block, 1)
    two, six = z_shift(block, -2), z_shift(block, 2)
    return one, two, six, seven


def gather_z_far(two, six):
    three, five = z_shift(two, -1), z_shift(six, 1)
    low, high = z_shift(six[:TILE], 2), z_shift(two[TILE:], -2)
    return jnp.concatenate([three, low, high, five])


def backward_kernel(
    place, count, where, values, own_near, other_near, own_far, other_far, piece, back, held, total
):
    total[...] = jnp.zeros_like(total)

    def slot(k, carry):
        mine, distance, y = locate(place[k, 0], where)
        far = (distance >= FAR[0]) & (distance <= FAR[-1])
        index = jnp.where(distance < FAR[0], distance, distance - len(FAR)) * YL + y
        for source, good in (
            (own_near, mine & ~far),
            (other_near, ~mine & ~far),
            (own_far, mine & far),
            (other_far, ~mine & far),
        ):

            @pl.when(good)
            def _():
                held[...] = source[index]

        total[place[k, 1]] += dot3(split(values[k]), split(held[...]), ((0,), (0,)))
        return carry

    lax.fori_loop(0, count[0], slot, 0)
    for j in range(back.shape[0]):
        back[j, :TILE, :] = total[j]
        back[j, TILE:, :] = piece[...]


def backward(place, count, where, values, near, other_near, far, other_far, piece, tiles):
    width = near.shape[-1]
    return pl.pallas_call(
        backward_kernel,
        out_shape=shaped(tiles, TILE + piece.shape[0], width),
        in_specs=[SMEM] * 3 + [VMEM] * 6,
        out_specs=VMEM,
        scratch_shapes=[
            pltpu.VMEM((TILE, width), jnp.float32),
            pltpu.VMEM((tiles, TILE, width), jnp.float32),
        ],
        compiler_params=params(24),
        name="backward_tiles",
    )(place, count, where, values, near, other_near, far, other_far, piece)


def final_kernel(parts, weight, result, weight_grad, bias_grad):
    back = parts[0, :TILE, :]
    for j in range(1, parts.shape[0]):
        back = back + parts[j, :TILE, :]
    result[...] = dot3(split(back), split(weight[...]), ((1,), (1,)))
    rows = parts.shape[1] - TILE - 8
    for j in range(parts.shape[0]):
        weight_grad[j * rows : (j + 1) * rows, :] = parts[j, TILE : TILE + rows, :]
    bias_grad[...] = parts[0, TILE + rows : TILE + rows + 1, :]


def final(parts, weight):
    return pl.pallas_call(
        final_kernel,
        out_shape=(
            shaped(TILE, weight.shape[0]),
            shaped(*weight.shape),
            shaped(1, weight.shape[1]),
        ),
        in_specs=[VMEM, VMEM],
        out_specs=(VMEM,) * 3,
        compiler_params=params(16),
        name="final",
    )(parts, weight)


def body(node_features, weight, bias, tile_values, tile_coords, tile_count, cotangent):
    values = tile_values[0, 0]
    place = tile_coords[0, 0]
    count = tile_count.reshape(1)
    local_nodes, width = node_features.shape
    row_count = lax.axis_size("row")
    col_count = lax.axis_size("col")
    factor = 1.0 / math.sqrt(local_nodes * row_count * col_count)
    col = lax.axis_index("col")
    where = jnp.stack([lax.div(col, 2 * YL), lax.rem(lax.div(col, 2), YL), lax.rem(col, 2)])

    features = lax.all_to_all(
        jnp.broadcast_to(node_features[None], (row_count, local_nodes, width)), "row", 0, 0
    )
    keep, send = forward(place, count, where, values, features)
    cot_other = lax.ppermute(cotangent, "col", Y_SWAP)
    summed = scatter_z(*add_cores(keep, lax.ppermute(send, "col", CORE_SWAP)))
    summed, cot_other = lax.optimization_barrier((summed, cot_other))
    summed_other = lax.ppermute(summed, "col", Y_SWAP)
    output, grads, extra = middle(
        where, summed, summed_other, weight, bias.reshape(1, width), cotangent, cot_other, row_count
    )

    one, two, six, seven = gather_z(grads)
    piece = jnp.sum(lax.all_to_all(extra, "row", 0, 0), axis=0)
    piece, one, two, six, seven = lax.optimization_barrier((piece, one, two, six, seven))
    far = gather_z_far(two, six)
    near = jnp.concatenate([grads, one, two, six, seven])
    other_near = lax.ppermute(near, "col", CORE_SWAP)
    piece = piece + lax.ppermute(piece, "col", CORE_SWAP)
    pieces = jnp.broadcast_to(piece[None], (Z,) + piece.shape)
    pieces = lax.all_to_all(pieces, "col", 0, 0, axis_index_groups=Z_GROUPS)
    piece = jnp.sum(pieces, axis=0) * factor
    piece, far = lax.optimization_barrier((piece, far))
    other_far = lax.ppermute(far, "col", CORE_SWAP)

    def tiles(value):
        return value.reshape(-1, TILE, width)

    back = backward(
        place, count, where, values, tiles(near), tiles(other_near), tiles(far), tiles(other_far),
        piece, row_count,
    )
    parts = lax.all_to_all(back, "row", 0, 0)
    input_grad, weight_grad, bias_grad = final(parts, weight)
    return (output, input_grad, weight_grad, bias_grad.reshape(width))


def solution(mesh):
    in_specs = (
        P(("col", "row"), None),
        P(),
        P(),
        P("row", "col", None, None, None),
        P("row", "col", None, None),
        P("row", "col"),
        P(("row", "col"), None),
    )
    out_specs = (P(("row", "col"), None), P(("col", "row"), None), P(), P())
    return jax.shard_map(body, mesh=mesh, in_specs=in_specs, out_specs=out_specs, check_vma=False)
```

```python
import functools
import math

import jax
import jax.numpy as jnp
from jax import lax
from jax.experimental import pallas as pl
from jax.experimental.pallas import tpu as pltpu
from jax.sharding import PartitionSpec as P

Z, YL = 8, 2
TILE = 128
PAIR = YL * TILE
JOIN_COST = 10**12
HALVES_COST = 10**12


def col_pairs(move):
    pairs = []
    for z in range(Z):
        for y in range(YL):
            for core in range(2):
                a, b, c = move(z, y, core)
                pairs.append(((z * YL + y) * 2 + core, (a * YL + b) * 2 + c))
    return pairs


CORE_SWAP = col_pairs(lambda z, y, core: (z, y, 1 - core))
Y_SWAP = col_pairs(lambda z, y, core: (z, 1 - y, core))
Z_GROUPS = [[(z * YL + y) * 2 + core for z in range(Z)] for y in range(YL) for core in range(2)]


def z_shift(value, distance):
    return lax.ppermute(value, "col", col_pairs(lambda z, y, core: ((z + distance) % Z, y, core)))


SMEM = pl.BlockSpec(memory_space=pltpu.SMEM)
VMEM = pl.BlockSpec(memory_space=pltpu.VMEM)


def params(mib):
    return pltpu.CompilerParams(vmem_limit_bytes=mib * 1024 * 1024)


def shaped(*shape):
    return jax.ShapeDtypeStruct(shape, jnp.float32)


def split(value):
    high = value.astype(jnp.bfloat16)
    low = (value - high.astype(jnp.float32)).astype(jnp.bfloat16)
    return high, low


def dot3(left, right, contract):
    def one(a, b):
        return lax.dot_general(a, b, (contract, ((), ())), preferred_element_type=jnp.float32)

    return one(left[0], right[0]) + (one(left[0], right[1]) + one(left[1], right[0]))


def locate(tile, where):
    mine = lax.rem(tile, 2) == where[2]
    distance = lax.rem(lax.div(tile, 2 * YL) - where[0] + Z, Z)
    return mine, distance, lax.rem(lax.div(tile, 2), YL)


def broadcast_kernel(block, out):
    for j in range(out.shape[0]):
        out[j] = block[...]


def broadcast(block, copies):
    return pl.pallas_call(
        broadcast_kernel,
        out_shape=shaped(copies, *block.shape),
        in_specs=[VMEM],
        out_specs=VMEM,
        compiler_params=params(3),
        name="broadcast_rows",
    )(block)


def forward_kernel(place, count, where, values, features, keep, send, high, low):
    keep[...] = jnp.zeros_like(keep)
    send[...] = jnp.zeros_like(send)
    for j in range(features.shape[0]):
        high[j], low[j] = split(features[j])
    for k in range(values.shape[0]):
        col = place[k, 1]
        mine, distance, y = locate(place[k, 0], where)
        live = k < count[0]
        product = dot3(split(values[k]), (high[col], low[col]), ((1,), (0,)))
        index = distance * YL + y
        keep[index] += jnp.where(live & mine, product, 0.0)
        send[index] += jnp.where(live & ~mine, product, 0.0)


def forward(place, count, where, values, features):
    tiles = Z * YL
    width = features.shape[-1]
    return pl.pallas_call(
        forward_kernel,
        out_shape=(shaped(tiles, TILE, width),) * 2,
        in_specs=[SMEM, SMEM, SMEM, VMEM, VMEM],
        out_specs=(VMEM,) * 2,
        scratch_shapes=[
            pltpu.VMEM(features.shape, jnp.bfloat16),
            pltpu.VMEM(features.shape, jnp.bfloat16),
        ],
        compiler_params=params(12),
        name="forward_tiles",
    )(place, count, where, values, features)


def add_cores_kernel(first, second, own, one, two, three, four_up, four_down, five, six, seven):
    def total(tile):
        return first[tile] + second[tile]

    for distance, out in ((3, three), (5, five), (0, own), (1, one), (2, two), (6, six), (7, seven)):
        for y in range(YL):
            out[y * TILE : (y + 1) * TILE, :] = total(distance * YL + y)
    four_up[...] = total(4 * YL)
    four_down[...] = total(4 * YL + 1)


def add_cores(first, second):
    width = first.shape[-1]
    whole, half = shaped(PAIR, width), shaped(TILE, width)
    return pl.pallas_call(
        add_cores_kernel,
        out_shape=(whole,) * 4 + (half,) * 2 + (whole,) * 3,
        in_specs=[VMEM] * 2,
        out_specs=(VMEM,) * 9,
        compiler_params=params(10),
        name="add_cores",
    )(first, second)


def relay_kernel(two, three, four_up, six, five, four_down, up, down):
    up[:TILE, :] = two[:TILE, :] + three[:TILE, :] + four_up[...]
    up[TILE:, :] = two[TILE:, :] + three[TILE:, :]
    down[:TILE, :] = six[:TILE, :] + five[:TILE, :]
    down[TILE:, :] = six[TILE:, :] + five[TILE:, :] + four_down[...]


def relay(*operands):
    return pl.pallas_call(
        relay_kernel,
        out_shape=(jax.ShapeDtypeStruct(operands[0].shape, jnp.float32),) * 2,
        in_specs=[VMEM] * 6,
        out_specs=(VMEM,) * 2,
        compiler_params=params(5),
        name="relay",
    )(*operands)


def scatter_z(own, one, two, three, four_up, four_down, five, six, seven):
    from_three, from_five = z_shift(three, 1), z_shift(five, -1)
    from_up, from_down = z_shift(four_up, 2), z_shift(four_down, -2)
    from_one, from_seven = z_shift(one, 1), z_shift(seven, -1)
    up, down = relay(two, from_three, from_up, six, from_five, from_down)
    from_two, from_six = z_shift(up, 2), z_shift(down, -2)
    return ((own + from_one) + from_seven) + (from_two + from_six)


def middle_kernel(where, mine, other, weight, bias, cot_own, cot_other, output, grad, total, cots):
    y = where[1]
    cots[y] = cot_own[...]
    cots[1 - y] = cot_other[...]
    cot = cots[...].reshape(grad.shape)
    summed = mine[...] + other[...]
    total[...] = summed
    pre = dot3(split(summed), split(weight[...]), ((1,), (0,))) + bias[...]
    sigma = jax.nn.sigmoid(pre)
    grad[...] = cot * (sigma * (1.0 + pre * (1.0 - sigma)))
    cots[...] = (pre * sigma).reshape(cots.shape)
    output[...] = cots[y]


def middle(where, mine, other, weight, bias, cot_own, cot_other):
    width = weight.shape[1]
    return pl.pallas_call(
        middle_kernel,
        out_shape=(shaped(TILE, width), shaped(PAIR, width), shaped(PAIR, weight.shape[0])),
        in_specs=[SMEM] + [VMEM] * 6,
        out_specs=(VMEM,) * 3,
        scratch_shapes=[pltpu.VMEM((YL, TILE, width), jnp.float32)],
        compiler_params=params(6),
        name="middle",
    )(where, mine, other, weight, bias, cot_own, cot_other)


def outer_kernel(total, grad, extra):
    value = grad[...]
    sums = jnp.broadcast_to(jnp.sum(value, axis=0, keepdims=True), (8, value.shape[1]))
    product = dot3(split(total[...]), split(value), ((0,), (0,)))
    pieces = extra.shape[0]
    rows = product.shape[0] // pieces
    for j in range(pieces):
        extra[j, :rows, :] = product[j * rows : (j + 1) * rows, :]
        extra[j, rows:, :] = sums


def outer(total, grad, pieces):
    return pl.pallas_call(
        outer_kernel,
        out_shape=shaped(pieces, total.shape[1] // pieces + 8, grad.shape[1]),
        in_specs=[VMEM] * 2,
        out_specs=VMEM,
        compiler_params=params(4),
        name="outer",
    )(total, grad)


def spread_kernel(parts, out):
    piece = parts[0]
    for j in range(1, parts.shape[0]):
        piece = piece + parts[j]
    for j in range(out.shape[0]):
        out[j] = piece


def spread(parts, copies):
    return pl.pallas_call(
        spread_kernel,
        out_shape=shaped(copies, *parts.shape[1:]),
        in_specs=[VMEM],
        out_specs=VMEM,
        compiler_params=params(3),
        name="spread",
    )(parts)


def halves_kernel(two, six, low, high):
    low[...] = six[:TILE, :]
    high[...] = two[TILE:, :]


def halves(two, six):
    return pl.pallas_call(
        halves_kernel,
        out_shape=(shaped(TILE, two.shape[1]),) * 2,
        in_specs=[VMEM] * 2,
        out_specs=(VMEM,) * 2,
        compiler_params=params(3),
        cost_estimate=pl.CostEstimate(flops=HALVES_COST, bytes_accessed=0, transcendentals=0),
        name="halves",
    )(two, six)


def join_kernel(*refs):
    out = refs[-1]
    start = 0
    for part in refs[:-1]:
        out[start : start + part.shape[0], :] = part[...]
        start += part.shape[0]


def join(*blocks):
    rows, width = sum(block.shape[0] for block in blocks), blocks[0].shape[1]
    return pl.pallas_call(
        join_kernel,
        out_shape=shaped(rows, width),
        in_specs=[VMEM] * len(blocks),
        out_specs=VMEM,
        compiler_params=params(8),
        cost_estimate=pl.CostEstimate(flops=JOIN_COST, bytes_accessed=0, transcendentals=0),
        name="join",
    )(*blocks)


def total_kernel(parts, out, *, factor):
    piece = parts[0]
    for j in range(1, parts.shape[0]):
        piece = piece + parts[j]
    out[...] = piece * factor


def total_of(parts, factor):
    return pl.pallas_call(
        functools.partial(total_kernel, factor=factor),
        out_shape=shaped(*parts.shape[1:]),
        in_specs=[VMEM],
        out_specs=VMEM,
        compiler_params=params(3),
        name="total",
    )(parts)


def backward_kernel(place, count, where, values, own, other, piece, piece_other, back):
    back[...] = jnp.zeros_like(back)
    for k in range(values.shape[0]):
        mine, distance, y = locate(place[k, 0], where)
        rows = pl.ds(pl.multiple_of((distance * YL + y) * TILE, TILE), TILE)
        block = jnp.where(mine, own[rows, :], other[rows, :])
        product = dot3(split(values[k]), split(block), ((0,), (0,)))
        back[place[k, 1], :TILE, :] += jnp.where(k < count[0], product, 0.0)
    both = piece[...] + piece_other[...]
    for j in range(back.shape[0]):
        back[j, TILE:, :] = both


def backward(place, count, where, values, own, other, piece, piece_other, tiles):
    return pl.pallas_call(
        backward_kernel,
        out_shape=shaped(tiles, TILE + piece.shape[0], own.shape[1]),
        in_specs=[SMEM] * 3 + [VMEM] * 5,
        out_specs=VMEM,
        compiler_params=params(12),
        name="backward_tiles",
    )(place, count, where, values, own, other, piece, piece_other)


def final_kernel(parts, weight, result, weight_grad, bias_grad):
    back = parts[0, :TILE, :]
    for j in range(1, parts.shape[0]):
        back = back + parts[j, :TILE, :]
    result[...] = dot3(split(back), split(weight[...]), ((1,), (1,)))
    rows = parts.shape[1] - TILE - 8
    for j in range(parts.shape[0]):
        weight_grad[j * rows : (j + 1) * rows, :] = parts[j, TILE : TILE + rows, :]
    bias_grad[...] = parts[0, TILE + rows : TILE + rows + 1, :]


def final(parts, weight):
    return pl.pallas_call(
        final_kernel,
        out_shape=(
            shaped(TILE, weight.shape[0]),
            shaped(*weight.shape),
            shaped(1, weight.shape[1]),
        ),
        in_specs=[VMEM, VMEM],
        out_specs=(VMEM,) * 3,
        compiler_params=params(5),
        name="final",
    )(parts, weight)


def body(node_features, weight, bias, tile_values, tile_coords, tile_count, cotangent):
    values = tile_values[0, 0]
    local_nodes, width = node_features.shape
    row_count = lax.axis_size("row")
    col_count = lax.axis_size("col")
    factor = 1.0 / math.sqrt(local_nodes * row_count * col_count)

    features = lax.all_to_all(broadcast(node_features, row_count), "row", 0, 0)
    features, tile_coords, tile_count, col = lax.optimization_barrier(
        (features, tile_coords, tile_count, lax.axis_index("col"))
    )
    place, count = tile_coords[0, 0], tile_count.reshape(1)
    where = jnp.stack([lax.div(col, 2 * YL), lax.rem(lax.div(col, 2), YL), lax.rem(col, 2)])
    keep, send = forward(place, count, where, values, features)
    cot_other = lax.ppermute(cotangent, "col", Y_SWAP)
    summed = scatter_z(*add_cores(keep, lax.ppermute(send, "col", CORE_SWAP)))
    summed, cot_other = lax.optimization_barrier((summed, cot_other))
    summed_other = lax.ppermute(summed, "col", Y_SWAP)
    output, grads, total = middle(
        where, summed, summed_other, weight, bias.reshape(1, width), cotangent, cot_other
    )

    two, six = z_shift(grads, -2), z_shift(grads, 2)
    one, seven = z_shift(grads, -1), z_shift(grads, 1)
    parts = lax.all_to_all(outer(total, grads, row_count), "row", 0, 0)
    parts = lax.all_to_all(spread(parts, Z), "col", 0, 0, axis_index_groups=Z_GROUPS)
    three, five = z_shift(two, -1), z_shift(six, 1)
    low, high = halves(two, six)
    low, high = z_shift(low, 2), z_shift(high, -2)
    own = join(grads, one, two, three, low, high, five, six, seven)
    piece = total_of(parts, factor)
    own, piece = lax.optimization_barrier((own, piece))
    other = lax.ppermute(own, "col", CORE_SWAP)
    piece_other = lax.ppermute(piece, "col", CORE_SWAP)
    back = backward(place, count, where, values, own, other, piece, piece_other, row_count)
    parts = lax.all_to_all(back, "row", 0, 0)
    input_grad, weight_grad, bias_grad = final(parts, weight)
    return (output, input_grad, weight_grad, bias_grad.reshape(width))


def solution(mesh):
    in_specs = (
        P(("col", "row"), None),
        P(),
        P(),
        P("row", "col", None, None, None),
        P("row", "col", None, None),
        P("row", "col"),
        P(("row", "col"), None),
    )
    out_specs = (P(("row", "col"), None), P(("col", "row"), None), P(), P())
    return jax.shard_map(body, mesh=mesh, in_specs=in_specs, out_specs=out_specs, check_vma=False)
```

```python
import functools
import math

import jax
import jax.numpy as jnp
from jax import lax
from jax.experimental import pallas as pl
from jax.experimental.pallas import tpu as pltpu
from jax.sharding import PartitionSpec as P

Z, YL = 8, 2
X, YH = 4, 2
TILE = 128
PAIR = YL * TILE
JOIN_COST = 10**12
HALVES_COST = 10**12
ROWS_COST = 10**12
UNPACK_COST = 10**10
SUMS_COST = 10**10
JOIN_PARTS = 4


def col_pairs(move):
    pairs = []
    for z in range(Z):
        for y in range(YL):
            for core in range(2):
                a, b, c = move(z, y, core)
                pairs.append(((z * YL + y) * 2 + core, (a * YL + b) * 2 + c))
    return pairs


CORE_SWAP = col_pairs(lambda z, y, core: (z, y, 1 - core))
Y_SWAP = col_pairs(lambda z, y, core: (z, 1 - y, core))
Z_GROUPS = [[(z * YL + y) * 2 + core for z in range(Z)] for y in range(YL) for core in range(2)]


def z_shift(value, distance):
    return lax.ppermute(value, "col", col_pairs(lambda z, y, core: ((z + distance) % Z, y, core)))


def row_pairs(move):
    pairs = []
    for x in range(X):
        for h in range(YH):
            a, b = move(x, h)
            pairs.append((x * YH + h, (a % X) * YH + b))
    return pairs


def x_shift(value, distance):
    return lax.ppermute(value, "row", row_pairs(lambda x, h: (x + distance, h)))


def h_swap(value):
    return lax.ppermute(value, "row", row_pairs(lambda x, h: (x, 1 - h)))


SMEM = pl.BlockSpec(memory_space=pltpu.SMEM)
VMEM = pl.BlockSpec(memory_space=pltpu.VMEM)


def params(mib):
    return pltpu.CompilerParams(vmem_limit_bytes=mib * 1024 * 1024)


def shaped(*shape):
    return jax.ShapeDtypeStruct(shape, jnp.float32)


def split(value):
    high = value.astype(jnp.bfloat16)
    low = (value - high.astype(jnp.float32)).astype(jnp.bfloat16)
    return high, low


def dot3(left, right, contract):
    def one(a, b):
        return lax.dot_general(a, b, (contract, ((), ())), preferred_element_type=jnp.float32)

    return one(left[0], right[0]) + (one(left[0], right[1]) + one(left[1], right[0]))


def locate(tile, where):
    mine = lax.rem(tile, 2) == where[2]
    distance = lax.rem(lax.div(tile, 2 * YL) - where[0] + Z, Z)
    return mine, distance, lax.rem(lax.div(tile, 2), YL)


def halve_kernel(*refs):
    count = len(refs) - 2
    for j in range(count):
        refs[count][j], refs[count + 1][j] = split(refs[j][...])


def halve(*blocks):
    shape = jax.ShapeDtypeStruct((len(blocks),) + blocks[0].shape, jnp.bfloat16)
    return pl.pallas_call(
        halve_kernel,
        out_shape=(shape, shape),
        in_specs=[VMEM] * len(blocks),
        out_specs=(VMEM,) * 2,
        compiler_params=params(3),
        cost_estimate=pl.CostEstimate(flops=ROWS_COST, bytes_accessed=0, transcendentals=0),
        name="halve",
    )(*blocks)


def row_index(tile, where):
    across = lax.rem(lax.rem(tile, YH) + where[4], YH)
    return across * X + lax.rem(lax.div(tile, YH) - where[3] + X, X)


def forward_kernel(place, count, where, values, near_high, near_low, a, b, c, d, keep, send, high, low):
    keep[...] = jnp.zeros_like(keep)
    send[...] = jnp.zeros_like(send)
    for j, part in enumerate((a, b, c, d)):
        high[j], low[j] = near_high[j], near_low[j]
        high[X + j], low[X + j] = split(part[...])
    for k in range(values.shape[0]):
        col = row_index(place[k, 1], where)
        mine, distance, y = locate(place[k, 0], where)
        live = k < count[0]
        product = dot3(split(values[k]), (high[col], low[col]), ((1,), (0,)))
        index = distance * YL + y
        keep[index] += jnp.where(live & mine, product, 0.0)
        send[index] += jnp.where(live & ~mine, product, 0.0)


def forward(place, count, where, values, near, far):
    tiles = Z * YL
    width = far[0].shape[-1]
    parts = pltpu.VMEM((X * YH, TILE, width), jnp.bfloat16)
    return pl.pallas_call(
        forward_kernel,
        out_shape=(shaped(tiles, TILE, width),) * 2,
        in_specs=[SMEM, SMEM, SMEM] + [VMEM] * 7,
        out_specs=(VMEM,) * 2,
        scratch_shapes=[parts, parts],
        compiler_params=params(12),
        name="forward_tiles",
    )(place, count, where, values, *near, *far)


def add_cores_kernel(first, second, own, one, two, three, four_up, four_down, five, six, seven):
    def total(tile):
        return first[tile] + second[tile]

    for distance, out in ((3, three), (5, five), (0, own), (1, one), (2, two), (6, six), (7, seven)):
        for y in range(YL):
            out[y * TILE : (y + 1) * TILE, :] = total(distance * YL + y)
    four_up[...] = total(4 * YL)
    four_down[...] = total(4 * YL + 1)


def add_cores(first, second):
    width = first.shape[-1]
    whole, half = shaped(PAIR, width), shaped(TILE, width)
    return pl.pallas_call(
        add_cores_kernel,
        out_shape=(whole,) * 4 + (half,) * 2 + (whole,) * 3,
        in_specs=[VMEM] * 2,
        out_specs=(VMEM,) * 9,
        compiler_params=params(10),
        name="add_cores",
    )(first, second)


def relay_kernel(two, three, four_up, six, five, four_down, up, down):
    up[:TILE, :] = two[:TILE, :] + three[:TILE, :] + four_up[...]
    up[TILE:, :] = two[TILE:, :] + three[TILE:, :]
    down[:TILE, :] = six[:TILE, :] + five[:TILE, :]
    down[TILE:, :] = six[TILE:, :] + five[TILE:, :] + four_down[...]


def relay(*operands):
    return pl.pallas_call(
        relay_kernel,
        out_shape=(jax.ShapeDtypeStruct(operands[0].shape, jnp.float32),) * 2,
        in_specs=[VMEM] * 6,
        out_specs=(VMEM,) * 2,
        compiler_params=params(5),
        name="relay",
    )(*operands)


def scatter_z(own, one, two, three, four_up, four_down, five, six, seven):
    from_three, from_five = z_shift(three, 1), z_shift(five, -1)
    from_up, from_down = z_shift(four_up, 2), z_shift(four_down, -2)
    from_one, from_seven = z_shift(one, 1), z_shift(seven, -1)
    up, down = relay(two, from_three, from_up, six, from_five, from_down)
    from_two, from_six = z_shift(up, 2), z_shift(down, -2)
    return ((own + from_one) + from_seven) + (from_two + from_six)


def middle_kernel(where, mine, other, weight, bias, cot_own, cot_other, output, grad, total, cots):
    y = where[1]
    cots[y] = cot_own[...]
    cots[1 - y] = cot_other[...]
    cot = cots[...].reshape(grad.shape)
    summed = mine[...] + other[...]
    total[...] = summed
    pre = dot3(split(summed), split(weight[...]), ((1,), (0,))) + bias[...]
    sigma = jax.nn.sigmoid(pre)
    grad[...] = cot * (sigma * (1.0 + pre * (1.0 - sigma)))
    cots[...] = (pre * sigma).reshape(cots.shape)
    output[...] = cots[y]


def middle(where, mine, other, weight, bias, cot_own, cot_other):
    width = weight.shape[1]
    return pl.pallas_call(
        middle_kernel,
        out_shape=(shaped(TILE, width), shaped(PAIR, width), shaped(PAIR, weight.shape[0])),
        in_specs=[SMEM] + [VMEM] * 6,
        out_specs=(VMEM,) * 3,
        scratch_shapes=[pltpu.VMEM((YL, TILE, width), jnp.float32)],
        compiler_params=params(6),
        name="middle",
    )(where, mine, other, weight, bias, cot_own, cot_other)


def outer_kernel(total, grad, extra):
    value = grad[...]
    sums = jnp.broadcast_to(jnp.sum(value, axis=0, keepdims=True), (8, value.shape[1]))
    product = dot3(split(total[...]), split(value), ((0,), (0,)))
    pieces = extra.shape[0]
    rows = product.shape[0] // pieces
    for j in range(pieces):
        extra[j, :rows, :] = product[j * rows : (j + 1) * rows, :]
        extra[j, rows:, :] = sums


def outer(total, grad, pieces):
    return pl.pallas_call(
        outer_kernel,
        out_shape=shaped(pieces, total.shape[1] // pieces + 8, grad.shape[1]),
        in_specs=[VMEM] * 2,
        out_specs=VMEM,
        compiler_params=params(4),
        name="outer",
    )(total, grad)


def spread_kernel(parts, out):
    piece = parts[0]
    for j in range(1, parts.shape[0]):
        piece = piece + parts[j]
    for j in range(out.shape[0]):
        out[j] = piece


def spread(parts, copies):
    return pl.pallas_call(
        spread_kernel,
        out_shape=shaped(copies, *parts.shape[1:]),
        in_specs=[VMEM],
        out_specs=VMEM,
        compiler_params=params(3),
        name="spread",
    )(parts)


def halves_kernel(two, six, low, high):
    low[...] = six[:TILE, :]
    high[...] = two[TILE:, :]


def halves(two, six):
    return pl.pallas_call(
        halves_kernel,
        out_shape=(shaped(TILE, two.shape[1]),) * 2,
        in_specs=[VMEM] * 2,
        out_specs=(VMEM,) * 2,
        compiler_params=params(3),
        cost_estimate=pl.CostEstimate(flops=HALVES_COST, bytes_accessed=0, transcendentals=0),
        name="halves",
    )(two, six)


def join_kernel(*refs):
    parts, outs = refs[:-JOIN_PARTS], refs[-JOIN_PARTS:]
    rows, start = outs[0].shape[0], 0
    for part in parts:
        size = part.shape[0]
        outs[start // rows][start % rows : start % rows + size, :] = part[...]
        start += size


def join(*blocks):
    rows, width = sum(block.shape[0] for block in blocks), blocks[0].shape[1]
    return pl.pallas_call(
        join_kernel,
        out_shape=(shaped(rows // JOIN_PARTS, width),) * JOIN_PARTS,
        in_specs=[VMEM] * len(blocks),
        out_specs=(VMEM,) * JOIN_PARTS,
        compiler_params=params(8),
        cost_estimate=pl.CostEstimate(flops=JOIN_COST, bytes_accessed=0, transcendentals=0),
        name="join",
    )(*blocks)


def total_kernel(parts, out, *, factor):
    piece = parts[0]
    for j in range(1, parts.shape[0]):
        piece = piece + parts[j]
    out[...] = piece * factor


def total_of(parts, factor):
    return pl.pallas_call(
        functools.partial(total_kernel, factor=factor),
        out_shape=shaped(*parts.shape[1:]),
        in_specs=[VMEM],
        out_specs=VMEM,
        compiler_params=params(3),
        name="total",
    )(parts)


def backward_kernel(place, count, where, values, *refs):
    own, other = refs[:JOIN_PARTS], refs[JOIN_PARTS : 2 * JOIN_PARTS]
    outs, total = refs[2 * JOIN_PARTS : -1], refs[-1]
    total[...] = jnp.zeros_like(total)
    tiles = own[0].shape[0] // TILE
    for k in range(values.shape[0]):
        mine, distance, y = locate(place[k, 0], where)
        index = distance * YL + y
        rows = pl.ds(pl.multiple_of(lax.rem(index, tiles) * TILE, TILE), TILE)
        block = jnp.where(mine, own[0][rows, :], other[0][rows, :])
        for j in range(1, JOIN_PARTS):
            later = jnp.where(mine, own[j][rows, :], other[j][rows, :])
            block = jnp.where(index >= j * tiles, later, block)
        product = dot3(split(values[k]), split(block), ((0,), (0,)))
        total[row_index(place[k, 1], where)] += jnp.where(k < count[0], product, 0.0)
    for j, out in enumerate(outs):
        out[...] = total[j]


def backward(place, count, where, values, own, other):
    width = own[0].shape[1]
    return pl.pallas_call(
        backward_kernel,
        out_shape=(shaped(TILE, width),) * (X * YH),
        in_specs=[SMEM] * 3 + [VMEM] * (1 + 2 * JOIN_PARTS),
        out_specs=(VMEM,) * (X * YH),
        scratch_shapes=[pltpu.VMEM((X * YH, TILE, width), jnp.float32)],
        compiler_params=params(12),
        name="backward_tiles",
    )(place, count, where, values, *own, *other)


def pack_kernel(one, two, three, piece, piece_across, *outs):
    rows = piece.shape[0]
    for part, out in zip((one, two, three), outs):
        out[:TILE, :] = part[...]
        out[TILE : TILE + rows, :] = piece[...]
        out[TILE + rows :, :] = piece_across[...]


def pack(one, two, three, piece, piece_across):
    rows, width = one.shape[0] + 2 * piece.shape[0], one.shape[1]
    return pl.pallas_call(
        pack_kernel,
        out_shape=(shaped(rows, width),) * 3,
        in_specs=[VMEM] * 5,
        out_specs=(VMEM,) * 3,
        compiler_params=params(4),
        name="pack",
    )(one, two, three, piece, piece_across)


def gather_sums_kernel(cross, one, two, three, out):
    out[...] = (cross[...] + one[...]) + (two[...] + three[...])


def gather_sums(*parts):
    return pl.pallas_call(
        gather_sums_kernel,
        out_shape=shaped(*parts[0].shape),
        in_specs=[VMEM] * 4,
        out_specs=VMEM,
        compiler_params=params(3),
        cost_estimate=pl.CostEstimate(flops=SUMS_COST, bytes_accessed=0, transcendentals=0),
        name="gather_sums",
    )(*parts)


def unpack_kernel(where, home, one, two, three, piece, piece_across, back, weight_grad, bias_grad):
    back[...] = (home[...] + one[:TILE, :]) + (two[:TILE, :] + three[:TILE, :])
    rows = weight_grad.shape[0] // (X * YH)
    step = rows + 8
    for distance, source in enumerate((None, three, two, one)):
        x = lax.rem(where[3] + distance, X)
        for across in range(YH):
            if source is None:
                value = (piece, piece_across)[across][:rows, :]
            else:
                start = TILE + across * step
                value = source[start : start + rows, :]
            index = x * YH + lax.rem(where[4] + across, YH)
            weight_grad[pl.ds(pl.multiple_of(index * rows, rows), rows), :] = value
    bias_grad[...] = piece[rows : rows + 1, :]


def unpack(where, home, one, two, three, piece, piece_across, shape):
    return pl.pallas_call(
        unpack_kernel,
        out_shape=(shaped(*home.shape), shaped(*shape), shaped(1, shape[1])),
        in_specs=[SMEM] + [VMEM] * 6,
        out_specs=(VMEM,) * 3,
        compiler_params=params(5),
        cost_estimate=pl.CostEstimate(flops=UNPACK_COST, bytes_accessed=0, transcendentals=0),
        name="unpack",
    )(where, home, one, two, three, piece, piece_across)


def final_kernel(back, partner, weight, result):
    result[...] = dot3(split(back[...] + partner[...]), split(weight[...]), ((1,), (1,)))


def final(back, partner, weight):
    return pl.pallas_call(
        final_kernel,
        out_shape=shaped(TILE, weight.shape[0]),
        in_specs=[VMEM] * 3,
        out_specs=VMEM,
        compiler_params=params(3),
        name="final",
    )(back, partner, weight)


def body(node_features, weight, bias, tile_values, tile_coords, tile_count, cotangent):
    values = tile_values[0, 0]
    local_nodes, width = node_features.shape
    row_count = lax.axis_size("row")
    col_count = lax.axis_size("col")
    factor = 1.0 / math.sqrt(local_nodes * row_count * col_count)

    place, count = tile_coords[0, 0], tile_count.reshape(1)
    row, col = lax.axis_index("row"), lax.axis_index("col")
    where = jnp.stack(
        [
            lax.div(col, 2 * YL),
            lax.rem(lax.div(col, 2), YL),
            lax.rem(col, 2),
            lax.div(row, YH),
            lax.rem(row, YH),
        ]
    )

    partner = h_swap(node_features)
    near = halve(
        node_features,
        x_shift(node_features, -1),
        x_shift(node_features, 2),
        x_shift(node_features, 1),
    )
    far = (partner, x_shift(partner, -1), x_shift(partner, 2), x_shift(partner, 1))
    keep, send = forward(place, count, where, values, near, far)
    cot_other = lax.ppermute(cotangent, "col", Y_SWAP)
    summed = scatter_z(*add_cores(keep, lax.ppermute(send, "col", CORE_SWAP)))
    summed, cot_other = lax.optimization_barrier((summed, cot_other))
    summed_other = lax.ppermute(summed, "col", Y_SWAP)
    output, grads, total = middle(
        where, summed, summed_other, weight, bias.reshape(1, width), cotangent, cot_other
    )

    two, six = z_shift(grads, -2), z_shift(grads, 2)
    one, seven = z_shift(grads, -1), z_shift(grads, 1)
    parts = lax.all_to_all(outer(total, grads, row_count), "row", 0, 0)
    parts = lax.all_to_all(spread(parts, Z), "col", 0, 0, axis_index_groups=Z_GROUPS)
    three, five = z_shift(two, -1), z_shift(six, 1)
    low, high = halves(two, six)
    low, high = z_shift(low, 2), z_shift(high, -2)
    own = join(grads, one, two, three, low, high, five, six, seven)
    other = [lax.ppermute(part, "col", CORE_SWAP) for part in own]
    piece = total_of(parts, factor)
    piece = piece + lax.ppermute(piece, "col", CORE_SWAP)
    piece_across = h_swap(piece)
    home, *near, cross, one, two, three = backward(place, count, where, values, own, other)
    near = pack(*near, piece, piece_across)
    sums = gather_sums(cross, x_shift(one, 1), x_shift(two, 2), x_shift(three, -1))
    near = [x_shift(part, distance) for part, distance in zip(near, (1, 2, -1))]
    back, weight_grad, bias_grad = unpack(where, home, *near, piece, piece_across, weight.shape)
    input_grad = final(back, h_swap(sums), weight)
    return (output, input_grad, weight_grad, bias_grad.reshape(width))


def solution(mesh):
    in_specs = (
        P(("col", "row"), None),
        P(),
        P(),
        P("row", "col", None, None, None),
        P("row", "col", None, None),
        P("row", "col"),
        P(("row", "col"), None),
    )
    out_specs = (P(("row", "col"), None), P(("col", "row"), None), P(), P())
    return jax.shard_map(body, mesh=mesh, in_specs=in_specs, out_specs=out_specs, check_vma=False)
```

```python
import functools
import math

import jax
import jax.numpy as jnp
from jax import lax
from jax.experimental import pallas as pl
from jax.experimental.pallas import tpu as pltpu
from jax.sharding import PartitionSpec as P

Z, YL = 8, 2
X, YH = 4, 2
TILE = 128
PAIR = YL * TILE
JOIN_COST = 10**12
HALVES_COST = 10**12
ROWS_COST = 10**12
UNPACK_COST = 10**10
SUMS_COST = 10**10
JOIN_PARTS = 4


def col_pairs(move):
    pairs = []
    for z in range(Z):
        for y in range(YL):
            for core in range(2):
                a, b, c = move(z, y, core)
                pairs.append(((z * YL + y) * 2 + core, (a * YL + b) * 2 + c))
    return pairs


CORE_SWAP = col_pairs(lambda z, y, core: (z, y, 1 - core))
Y_SWAP = col_pairs(lambda z, y, core: (z, 1 - y, core))
Z_GROUPS = [[(z * YL + y) * 2 + core for z in range(Z)] for y in range(YL) for core in range(2)]


def z_shift(value, distance):
    def move(z, y, core):
        return (z + (1 - 2 * core) * distance) % Z, y, core

    return lax.ppermute(value, "col", col_pairs(move))


def row_pairs(move):
    pairs = []
    for x in range(X):
        for h in range(YH):
            a, b = move(x, h)
            pairs.append((x * YH + h, (a % X) * YH + b))
    return pairs


def x_shift(value, distance):
    return lax.ppermute(value, "row", row_pairs(lambda x, h: (x + distance, h)))


def h_swap(value):
    return lax.ppermute(value, "row", row_pairs(lambda x, h: (x, 1 - h)))


SMEM = pl.BlockSpec(memory_space=pltpu.SMEM)
VMEM = pl.BlockSpec(memory_space=pltpu.VMEM)


def params(mib):
    return pltpu.CompilerParams(vmem_limit_bytes=mib * 1024 * 1024)


def shaped(*shape):
    return jax.ShapeDtypeStruct(shape, jnp.float32)


def split(value):
    high = value.astype(jnp.bfloat16)
    low = (value - high.astype(jnp.float32)).astype(jnp.bfloat16)
    return high, low


def dot3(left, right, contract):
    def one(a, b):
        return lax.dot_general(a, b, (contract, ((), ())), preferred_element_type=jnp.float32)

    return one(left[0], right[0]) + (one(left[0], right[1]) + one(left[1], right[0]))


def locate(tile, where):
    mine = lax.rem(tile, 2) == where[2]
    away = lax.div(tile, 2 * YL) - where[0]
    distance = lax.rem(jnp.where(lax.rem(tile, 2) == 0, away, -away) + Z, Z)
    return mine, distance, lax.rem(lax.div(tile, 2), YL)


def halve_kernel(*refs):
    count = len(refs) - 2
    for j in range(count):
        refs[count][j], refs[count + 1][j] = split(refs[j][...])


def halve(*blocks):
    shape = jax.ShapeDtypeStruct((len(blocks),) + blocks[0].shape, jnp.bfloat16)
    return pl.pallas_call(
        halve_kernel,
        out_shape=(shape, shape),
        in_specs=[VMEM] * len(blocks),
        out_specs=(VMEM,) * 2,
        compiler_params=params(3),
        cost_estimate=pl.CostEstimate(flops=ROWS_COST, bytes_accessed=0, transcendentals=0),
        name="halve",
    )(*blocks)


def row_index(tile, where):
    across = lax.rem(lax.rem(tile, YH) + where[4], YH)
    return across * X + lax.rem(lax.div(tile, YH) - where[3] + X, X)


def forward_kernel(place, count, where, values, near_high, near_low, a, b, c, d, keep, send, high, low):
    keep[...] = jnp.zeros_like(keep)
    send[...] = jnp.zeros_like(send)
    for j, part in enumerate((a, b, c, d)):
        high[j], low[j] = near_high[j], near_low[j]
        high[X + j], low[X + j] = split(part[...])
    for k in range(values.shape[0]):
        col = row_index(place[k, 1], where)
        mine, distance, y = locate(place[k, 0], where)
        live = k < count[0]
        product = dot3(split(values[k]), (high[col], low[col]), ((1,), (0,)))
        index = distance * YL + y
        keep[index] += jnp.where(live & mine, product, 0.0)
        send[index] += jnp.where(live & ~mine, product, 0.0)


def forward(place, count, where, values, near, far):
    tiles = Z * YL
    width = far[0].shape[-1]
    parts = pltpu.VMEM((X * YH, TILE, width), jnp.bfloat16)
    return pl.pallas_call(
        forward_kernel,
        out_shape=(shaped(tiles, TILE, width),) * 2,
        in_specs=[SMEM, SMEM, SMEM] + [VMEM] * 7,
        out_specs=(VMEM,) * 2,
        scratch_shapes=[parts, parts],
        compiler_params=params(12),
        name="forward_tiles",
    )(place, count, where, values, *near, *far)


def add_cores_kernel(first, second, *outs):
    for tile, out in enumerate(outs):
        out[...] = first[tile] + second[tile]


def add_cores(first, second):
    tiles = first.shape[0]
    return pl.pallas_call(
        add_cores_kernel,
        out_shape=(shaped(*first.shape[1:]),) * tiles,
        in_specs=[VMEM] * 2,
        out_specs=(VMEM,) * tiles,
        compiler_params=params(10),
        name="add_cores",
    )(first, second)


def ring_z(blocks):
    up, down = blocks[4], blocks[5]
    for step in (3, 2, 1):
        up = blocks[step] + z_shift(up, 1)
    for step in (6, 7):
        down = blocks[step] + z_shift(down, -1)
    return blocks[0], z_shift(up, 1), z_shift(down, -1)


def last_sum_kernel(*refs):
    out = refs[-1]
    for y in range(YL):
        part = refs[3 * y][...] + refs[3 * y + 1][...] + refs[3 * y + 2][...]
        out[y * TILE : (y + 1) * TILE, :] = part


def last_sum(*parts):
    return pl.pallas_call(
        last_sum_kernel,
        out_shape=shaped(PAIR, parts[0].shape[1]),
        in_specs=[VMEM] * len(parts),
        out_specs=VMEM,
        compiler_params=params(4),
        name="last_sum",
    )(*parts)


def middle_kernel(where, mine, other, weight, bias, cot_own, cot_other, output, grad, extra, cots):
    y = where[1]
    cots[y] = cot_own[...]
    cots[1 - y] = cot_other[...]
    cot = cots[...].reshape(grad.shape)
    summed = split(mine[...] + other[...])
    pre = dot3(summed, split(weight[...]), ((1,), (0,))) + bias[...]
    sigma = jax.nn.sigmoid(pre)
    value = cot * (sigma * (1.0 + pre * (1.0 - sigma)))
    grad[...] = value
    cots[...] = (pre * sigma).reshape(cots.shape)
    output[...] = cots[y]
    sums = jnp.broadcast_to(jnp.sum(value, axis=0, keepdims=True), (8, value.shape[1]))
    product = dot3(summed, split(value), ((0,), (0,)))
    pieces = extra.shape[0]
    rows = product.shape[0] // pieces
    for j in range(pieces):
        extra[j, :rows, :] = product[j * rows : (j + 1) * rows, :]
        extra[j, rows:, :] = sums


def middle(where, mine, other, weight, bias, cot_own, cot_other):
    depth, width = weight.shape
    return pl.pallas_call(
        middle_kernel,
        out_shape=(
            shaped(TILE, width),
            shaped(PAIR, width),
            shaped(X * YH, depth // (X * YH) + 8, width),
        ),
        in_specs=[SMEM] + [VMEM] * 6,
        out_specs=(VMEM,) * 3,
        scratch_shapes=[pltpu.VMEM((YL, TILE, width), jnp.float32)],
        compiler_params=params(6),
        name="middle",
    )(where, mine, other, weight, bias, cot_own, cot_other)


def spread_kernel(parts, out):
    piece = parts[0]
    for j in range(1, parts.shape[0]):
        piece = piece + parts[j]
    for j in range(out.shape[0]):
        out[j] = piece


def spread(parts, copies):
    return pl.pallas_call(
        spread_kernel,
        out_shape=shaped(copies, *parts.shape[1:]),
        in_specs=[VMEM],
        out_specs=VMEM,
        compiler_params=params(4),
        name="spread",
    )(parts)


def halves_kernel(two, six, low, high):
    low[...] = six[:TILE, :]
    high[...] = two[TILE:, :]


def halves(two, six):
    return pl.pallas_call(
        halves_kernel,
        out_shape=(shaped(TILE, two.shape[1]),) * 2,
        in_specs=[VMEM] * 2,
        out_specs=(VMEM,) * 2,
        compiler_params=params(3),
        cost_estimate=pl.CostEstimate(flops=HALVES_COST, bytes_accessed=0, transcendentals=0),
        name="halves",
    )(two, six)


def join_kernel(*refs):
    parts, outs = refs[:-JOIN_PARTS], refs[-JOIN_PARTS:]
    rows, start = outs[0].shape[0], 0
    for part in parts:
        size = part.shape[0]
        outs[start // rows][start % rows : start % rows + size, :] = part[...]
        start += size


def join(*blocks):
    rows, width = sum(block.shape[0] for block in blocks), blocks[0].shape[1]
    return pl.pallas_call(
        join_kernel,
        out_shape=(shaped(rows // JOIN_PARTS, width),) * JOIN_PARTS,
        in_specs=[VMEM] * len(blocks),
        out_specs=(VMEM,) * JOIN_PARTS,
        compiler_params=params(8),
        cost_estimate=pl.CostEstimate(flops=JOIN_COST, bytes_accessed=0, transcendentals=0),
        name="join",
    )(*blocks)


def total_kernel(parts, out, *, factor):
    piece = parts[0]
    for j in range(1, parts.shape[0]):
        piece = piece + parts[j]
    out[...] = piece * factor


def total_of(parts, factor):
    return pl.pallas_call(
        functools.partial(total_kernel, factor=factor),
        out_shape=shaped(*parts.shape[1:]),
        in_specs=[VMEM],
        out_specs=VMEM,
        compiler_params=params(3),
        name="total",
    )(parts)


def backward_kernel(place, count, where, values, *refs):
    own, other = refs[:JOIN_PARTS], refs[JOIN_PARTS : 2 * JOIN_PARTS]
    outs, total = refs[2 * JOIN_PARTS : -1], refs[-1]
    total[...] = jnp.zeros_like(total)
    tiles = own[0].shape[0] // TILE
    for k in range(values.shape[0]):
        mine, distance, y = locate(place[k, 0], where)
        index = distance * YL + y
        rows = pl.ds(pl.multiple_of(lax.rem(index, tiles) * TILE, TILE), TILE)
        block = jnp.where(mine, own[0][rows, :], other[0][rows, :])
        for j in range(1, JOIN_PARTS):
            later = jnp.where(mine, own[j][rows, :], other[j][rows, :])
            block = jnp.where(index >= j * tiles, later, block)
        product = dot3(split(values[k]), split(block), ((0,), (0,)))
        total[row_index(place[k, 1], where)] += jnp.where(k < count[0], product, 0.0)
    for j, out in enumerate(outs):
        out[...] = total[j]


def backward(place, count, where, values, own, other):
    width = own[0].shape[1]
    return pl.pallas_call(
        backward_kernel,
        out_shape=(shaped(TILE, width),) * (X * YH),
        in_specs=[SMEM] * 3 + [VMEM] * (1 + 2 * JOIN_PARTS),
        out_specs=(VMEM,) * (X * YH),
        scratch_shapes=[pltpu.VMEM((X * YH, TILE, width), jnp.float32)],
        compiler_params=params(12),
        name="backward_tiles",
    )(place, count, where, values, *own, *other)


def pack_kernel(one, two, three, piece, piece_across, *outs):
    rows = piece.shape[0]
    for part, out in zip((one, two, three), outs):
        out[:TILE, :] = part[...]
        out[TILE : TILE + rows, :] = piece[...]
        out[TILE + rows :, :] = piece_across[...]


def pack(one, two, three, piece, piece_across):
    rows, width = one.shape[0] + 2 * piece.shape[0], one.shape[1]
    return pl.pallas_call(
        pack_kernel,
        out_shape=(shaped(rows, width),) * 3,
        in_specs=[VMEM] * 5,
        out_specs=(VMEM,) * 3,
        compiler_params=params(4),
        name="pack",
    )(one, two, three, piece, piece_across)


def gather_sums_kernel(cross, one, two, three, out):
    out[...] = (cross[...] + one[...]) + (two[...] + three[...])


def gather_sums(*parts):
    return pl.pallas_call(
        gather_sums_kernel,
        out_shape=shaped(*parts[0].shape),
        in_specs=[VMEM] * 4,
        out_specs=VMEM,
        compiler_params=params(3),
        cost_estimate=pl.CostEstimate(flops=SUMS_COST, bytes_accessed=0, transcendentals=0),
        name="gather_sums",
    )(*parts)


def unpack_kernel(where, home, one, two, three, piece, piece_across, back, weight_grad, bias_grad):
    back[...] = (home[...] + one[:TILE, :]) + (two[:TILE, :] + three[:TILE, :])
    rows = weight_grad.shape[0] // (X * YH)
    step = rows + 8
    for distance, source in enumerate((None, three, two, one)):
        x = lax.rem(where[3] + distance, X)
        for across in range(YH):
            if source is None:
                value = (piece, piece_across)[across][:rows, :]
            else:
                start = TILE + across * step
                value = source[start : start + rows, :]
            index = x * YH + lax.rem(where[4] + across, YH)
            weight_grad[pl.ds(pl.multiple_of(index * rows, rows), rows), :] = value
    bias_grad[...] = piece[rows : rows + 1, :]


def unpack(where, home, one, two, three, piece, piece_across, shape):
    return pl.pallas_call(
        unpack_kernel,
        out_shape=(shaped(*home.shape), shaped(*shape), shaped(1, shape[1])),
        in_specs=[SMEM] + [VMEM] * 6,
        out_specs=(VMEM,) * 3,
        compiler_params=params(5),
        cost_estimate=pl.CostEstimate(flops=UNPACK_COST, bytes_accessed=0, transcendentals=0),
        name="unpack",
    )(where, home, one, two, three, piece, piece_across)


def final_kernel(back, partner, weight, result):
    result[...] = dot3(split(back[...] + partner[...]), split(weight[...]), ((1,), (1,)))


def final(back, partner, weight):
    return pl.pallas_call(
        final_kernel,
        out_shape=shaped(TILE, weight.shape[0]),
        in_specs=[VMEM] * 3,
        out_specs=VMEM,
        compiler_params=params(3),
        name="final",
    )(back, partner, weight)


def body(node_features, weight, bias, tile_values, tile_coords, tile_count, cotangent):
    values = tile_values[0, 0]
    local_nodes, width = node_features.shape
    row_count = lax.axis_size("row")
    col_count = lax.axis_size("col")
    factor = 1.0 / math.sqrt(local_nodes * row_count * col_count)

    place, count = tile_coords[0, 0], tile_count.reshape(1)
    row, col = lax.axis_index("row"), lax.axis_index("col")
    where = jnp.stack(
        [
            lax.div(col, 2 * YL),
            lax.rem(lax.div(col, 2), YL),
            lax.rem(col, 2),
            lax.div(row, YH),
            lax.rem(row, YH),
        ]
    )

    partner = h_swap(node_features)
    near = halve(
        node_features,
        x_shift(node_features, -1),
        x_shift(node_features, 2),
        x_shift(node_features, 1),
    )
    far = (partner, x_shift(partner, -1), x_shift(partner, 2), x_shift(partner, 1))
    keep, send = forward(place, count, where, values, near, far)
    cot_other = lax.ppermute(cotangent, "col", Y_SWAP)
    tiles = add_cores(keep, lax.ppermute(send, "col", CORE_SWAP))
    summed = last_sum(*ring_z(tiles[0::YL]), *ring_z(tiles[1::YL]))
    summed, cot_other = lax.optimization_barrier((summed, cot_other))
    summed_other = lax.ppermute(summed, "col", Y_SWAP)
    output, grads, extra = middle(
        where, summed, summed_other, weight, bias.reshape(1, width), cotangent, cot_other
    )

    two, six = z_shift(grads, -2), z_shift(grads, 2)
    one, seven = z_shift(grads, -1), z_shift(grads, 1)
    parts = lax.all_to_all(extra, "row", 0, 0)
    parts = lax.all_to_all(spread(parts, Z), "col", 0, 0, axis_index_groups=Z_GROUPS)
    three, five = z_shift(two, -1), z_shift(six, 1)
    low, high = halves(two, six)
    low, high = z_shift(low, 2), z_shift(high, -2)
    own = join(grads, one, two, three, low, high, five, six, seven)
    other = [lax.ppermute(part, "col", CORE_SWAP) for part in own]
    piece = total_of(parts, factor)
    piece = piece + lax.ppermute(piece, "col", CORE_SWAP)
    piece_across = h_swap(piece)
    home, *near, cross, one, two, three = backward(place, count, where, values, own, other)
    near = pack(*near, piece, piece_across)
    sums = gather_sums(cross, x_shift(one, 1), x_shift(two, 2), x_shift(three, -1))
    near = [x_shift(part, distance) for part, distance in zip(near, (1, 2, -1))]
    back, weight_grad, bias_grad = unpack(where, home, *near, piece, piece_across, weight.shape)
    input_grad = final(back, h_swap(sums), weight)
    return (output, input_grad, weight_grad, bias_grad.reshape(width))


def solution(mesh):
    in_specs = (
        P(("col", "row"), None),
        P(),
        P(),
        P("row", "col", None, None, None),
        P("row", "col", None, None),
        P("row", "col"),
        P(("row", "col"), None),
    )
    out_specs = (P(("row", "col"), None), P(("col", "row"), None), P(), P())
    return jax.shard_map(body, mesh=mesh, in_specs=in_specs, out_specs=out_specs, check_vma=False)
```

```python
import functools
import math

import jax
import jax.numpy as jnp
from jax import lax
from jax.experimental import pallas as pl
from jax.experimental.pallas import tpu as pltpu
from jax.sharding import PartitionSpec as P

Z, YL = 8, 2
X, YH = 4, 2
TILE = 128
PAIR = YL * TILE
FAR, NEAR = (3, 4, 5, 6), (7, 0, 1, 2)
JOIN_COST = 10**12
HALVES_COST = 10**12
ROWS_COST = 10**12
UNPACK_COST = 10**10
SUMS_COST = 10**10
JOIN_PARTS = 4


def col_pairs(move):
    pairs = []
    for z in range(Z):
        for y in range(YL):
            for core in range(2):
                a, b, c = move(z, y, core)
                pairs.append(((z * YL + y) * 2 + core, (a * YL + b) * 2 + c))
    return pairs


CORE_SWAP = col_pairs(lambda z, y, core: (z, y, 1 - core))
Y_SWAP = col_pairs(lambda z, y, core: (z, 1 - y, core))
Z_GROUPS = [[(z * YL + y) * 2 + core for z in range(Z)] for y in range(YL) for core in range(2)]


def z_shift(value, distance):
    def move(z, y, core):
        return (z + (2 * core - 1) * distance) % Z, y, core

    return lax.ppermute(value, "col", col_pairs(move))


def row_pairs(move):
    pairs = []
    for x in range(X):
        for h in range(YH):
            a, b = move(x, h)
            pairs.append((x * YH + h, (a % X) * YH + b))
    return pairs


def x_shift(value, distance):
    return lax.ppermute(value, "row", row_pairs(lambda x, h: (x + distance, h)))


def h_swap(value):
    return lax.ppermute(value, "row", row_pairs(lambda x, h: (x, 1 - h)))


SMEM = pl.BlockSpec(memory_space=pltpu.SMEM)
VMEM = pl.BlockSpec(memory_space=pltpu.VMEM)


def params(mib):
    return pltpu.CompilerParams(vmem_limit_bytes=mib * 1024 * 1024)


def shaped(*shape):
    return jax.ShapeDtypeStruct(shape, jnp.float32)


def split(value):
    high = value.astype(jnp.bfloat16)
    low = (value - high.astype(jnp.float32)).astype(jnp.bfloat16)
    return high, low


def dot3(left, right, contract):
    def one(a, b):
        return lax.dot_general(a, b, (contract, ((), ())), preferred_element_type=jnp.float32)

    return one(left[0], right[0]) + (one(left[0], right[1]) + one(left[1], right[0]))


def locate(tile, where):
    mine = lax.rem(tile, 2) == where[2]
    away = lax.div(tile, 2 * YL) - where[0]
    distance = lax.rem(jnp.where(lax.rem(tile, 2) == 0, -away, away) + Z, Z)
    return mine, distance, lax.rem(lax.div(tile, 2), YL)


def halve_kernel(*refs):
    count = len(refs) - 2
    for j in range(count):
        refs[count][j], refs[count + 1][j] = split(refs[j][...])


def halve(*blocks):
    shape = jax.ShapeDtypeStruct((len(blocks),) + blocks[0].shape, jnp.bfloat16)
    return pl.pallas_call(
        halve_kernel,
        out_shape=(shape, shape),
        in_specs=[VMEM] * len(blocks),
        out_specs=(VMEM,) * 2,
        compiler_params=params(3),
        cost_estimate=pl.CostEstimate(flops=ROWS_COST, bytes_accessed=0, transcendentals=0),
        name="halve",
    )(*blocks)


def row_index(tile, where):
    across = lax.rem(lax.rem(tile, YH) + where[4], YH)
    return across * X + lax.rem(lax.div(tile, YH) - where[3] + X, X)


def forward_kernel(
    place, count, where, values, near_high, near_low, a, b, c, d,
    keep_far, send_far, keep_near, send_near, high, low,
):
    for out in (keep_far, send_far, keep_near, send_near):
        out[...] = jnp.zeros_like(out)
    for j, part in enumerate((a, b, c, d)):
        high[j], low[j] = near_high[j], near_low[j]
        high[X + j], low[X + j] = split(part[...])
    for k in range(values.shape[0]):
        col = row_index(place[k, 1], where)
        mine, distance, y = locate(place[k, 0], where)
        live = k < count[0]
        product = dot3(split(values[k]), (high[col], low[col]), ((1,), (0,)))
        is_far = (distance >= FAR[0]) & (distance <= FAR[-1])
        far = jnp.where(is_far, distance - FAR[0], 0) * YL + y
        near = jnp.where(is_far, 0, lax.rem(distance + Z - NEAR[0], Z)) * YL + y
        keep_far[far] += jnp.where(live & mine & is_far, product, 0.0)
        send_far[far] += jnp.where(live & ~mine & is_far, product, 0.0)
        keep_near[near] += jnp.where(live & mine & ~is_far, product, 0.0)
        send_near[near] += jnp.where(live & ~mine & ~is_far, product, 0.0)


def forward(place, count, where, values, near, far):
    width = far[0].shape[-1]
    parts = pltpu.VMEM((X * YH, TILE, width), jnp.bfloat16)
    return pl.pallas_call(
        forward_kernel,
        out_shape=(shaped(len(FAR) * YL, TILE, width),) * 2
        + (shaped(len(NEAR) * YL, TILE, width),) * 2,
        in_specs=[SMEM, SMEM, SMEM] + [VMEM] * 7,
        out_specs=(VMEM,) * 4,
        scratch_shapes=[parts, parts],
        compiler_params=params(12),
        name="forward_tiles",
    )(place, count, where, values, *near, *far)


def add_cores_kernel(first, second, *outs):
    for tile, out in enumerate(outs):
        out[...] = first[tile] + second[tile]


def add_cores(first, second):
    tiles = first.shape[0]
    return pl.pallas_call(
        add_cores_kernel,
        out_shape=(shaped(*first.shape[1:]),) * tiles,
        in_specs=[VMEM] * 2,
        out_specs=(VMEM,) * tiles,
        compiler_params=params(10),
        name="add_cores",
    )(first, second)


def ring_z(blocks):
    up, down = blocks[4], blocks[5]
    for step in (3, 2, 1):
        up = blocks[step] + z_shift(up, 1)
    for step in (6, 7):
        down = blocks[step] + z_shift(down, -1)
    return blocks[0], z_shift(up, 1), z_shift(down, -1)


def last_sum_kernel(*refs):
    out = refs[-1]
    for y in range(YL):
        part = refs[3 * y][...] + refs[3 * y + 1][...] + refs[3 * y + 2][...]
        out[y * TILE : (y + 1) * TILE, :] = part


def last_sum(*parts):
    return pl.pallas_call(
        last_sum_kernel,
        out_shape=shaped(PAIR, parts[0].shape[1]),
        in_specs=[VMEM] * len(parts),
        out_specs=VMEM,
        compiler_params=params(4),
        name="last_sum",
    )(*parts)


def middle_kernel(where, mine, other, weight, bias, cot_own, cot_other, output, grad, extra, cots):
    y = where[1]
    cots[y] = cot_own[...]
    cots[1 - y] = cot_other[...]
    cot = cots[...].reshape(grad.shape)
    summed = split(mine[...] + other[...])
    pre = dot3(summed, split(weight[...]), ((1,), (0,))) + bias[...]
    sigma = jax.nn.sigmoid(pre)
    value = cot * (sigma * (1.0 + pre * (1.0 - sigma)))
    grad[...] = value
    cots[...] = (pre * sigma).reshape(cots.shape)
    output[...] = cots[y]
    sums = jnp.broadcast_to(jnp.sum(value, axis=0, keepdims=True), (8, value.shape[1]))
    product = dot3(summed, split(value), ((0,), (0,)))
    pieces = extra.shape[0]
    rows = product.shape[0] // pieces
    for j in range(pieces):
        extra[j, :rows, :] = product[j * rows : (j + 1) * rows, :]
        extra[j, rows:, :] = sums


def middle(where, mine, other, weight, bias, cot_own, cot_other):
    depth, width = weight.shape
    return pl.pallas_call(
        middle_kernel,
        out_shape=(
            shaped(TILE, width),
            shaped(PAIR, width),
            shaped(X * YH, depth // (X * YH) + 8, width),
        ),
        in_specs=[SMEM] + [VMEM] * 6,
        out_specs=(VMEM,) * 3,
        scratch_shapes=[pltpu.VMEM((YL, TILE, width), jnp.float32)],
        compiler_params=params(6),
        name="middle",
    )(where, mine, other, weight, bias, cot_own, cot_other)


def spread_kernel(parts, out):
    piece = parts[0]
    for j in range(1, parts.shape[0]):
        piece = piece + parts[j]
    for j in range(out.shape[0]):
        out[j] = piece


def spread(parts, copies):
    return pl.pallas_call(
        spread_kernel,
        out_shape=shaped(copies, *parts.shape[1:]),
        in_specs=[VMEM],
        out_specs=VMEM,
        compiler_params=params(4),
        name="spread",
    )(parts)


def halves_kernel(two, six, low, high):
    low[...] = six[:TILE, :]
    high[...] = two[TILE:, :]


def halves(two, six):
    return pl.pallas_call(
        halves_kernel,
        out_shape=(shaped(TILE, two.shape[1]),) * 2,
        in_specs=[VMEM] * 2,
        out_specs=(VMEM,) * 2,
        compiler_params=params(3),
        cost_estimate=pl.CostEstimate(flops=HALVES_COST, bytes_accessed=0, transcendentals=0),
        name="halves",
    )(two, six)


def join_kernel(*refs):
    parts, outs = refs[:-JOIN_PARTS], refs[-JOIN_PARTS:]
    rows, start = outs[0].shape[0], 0
    for part in parts:
        size = part.shape[0]
        outs[start // rows][start % rows : start % rows + size, :] = part[...]
        start += size


def join(*blocks):
    rows, width = sum(block.shape[0] for block in blocks), blocks[0].shape[1]
    return pl.pallas_call(
        join_kernel,
        out_shape=(shaped(rows // JOIN_PARTS, width),) * JOIN_PARTS,
        in_specs=[VMEM] * len(blocks),
        out_specs=(VMEM,) * JOIN_PARTS,
        compiler_params=params(8),
        cost_estimate=pl.CostEstimate(flops=JOIN_COST, bytes_accessed=0, transcendentals=0),
        name="join",
    )(*blocks)


def total_kernel(parts, out, *, factor):
    piece = parts[0]
    for j in range(1, parts.shape[0]):
        piece = piece + parts[j]
    out[...] = piece * factor


def total_of(parts, factor):
    return pl.pallas_call(
        functools.partial(total_kernel, factor=factor),
        out_shape=shaped(*parts.shape[1:]),
        in_specs=[VMEM],
        out_specs=VMEM,
        compiler_params=params(3),
        name="total",
    )(parts)


def backward_kernel(place, count, where, values, *refs):
    own, other = refs[:JOIN_PARTS], refs[JOIN_PARTS : 2 * JOIN_PARTS]
    outs, total = refs[2 * JOIN_PARTS : -1], refs[-1]
    total[...] = jnp.zeros_like(total)
    tiles = own[0].shape[0] // TILE
    for k in range(values.shape[0]):
        mine, distance, y = locate(place[k, 0], where)
        index = distance * YL + y
        rows = pl.ds(pl.multiple_of(lax.rem(index, tiles) * TILE, TILE), TILE)
        block = jnp.where(mine, own[0][rows, :], other[0][rows, :])
        for j in range(1, JOIN_PARTS):
            later = jnp.where(mine, own[j][rows, :], other[j][rows, :])
            block = jnp.where(index >= j * tiles, later, block)
        product = dot3(split(values[k]), split(block), ((0,), (0,)))
        total[row_index(place[k, 1], where)] += jnp.where(k < count[0], product, 0.0)
    for j, out in enumerate(outs):
        out[...] = total[j]


def backward(place, count, where, values, own, other):
    width = own[0].shape[1]
    return pl.pallas_call(
        backward_kernel,
        out_shape=(shaped(TILE, width),) * (X * YH),
        in_specs=[SMEM] * 3 + [VMEM] * (1 + 2 * JOIN_PARTS),
        out_specs=(VMEM,) * (X * YH),
        scratch_shapes=[pltpu.VMEM((X * YH, TILE, width), jnp.float32)],
        compiler_params=params(12),
        name="backward_tiles",
    )(place, count, where, values, *own, *other)


def pack_kernel(one, two, three, piece, piece_across, *outs):
    rows = piece.shape[0]
    for part, out in zip((one, two, three), outs):
        out[:TILE, :] = part[...]
        out[TILE : TILE + rows, :] = piece[...]
        out[TILE + rows :, :] = piece_across[...]


def pack(one, two, three, piece, piece_across):
    rows, width = one.shape[0] + 2 * piece.shape[0], one.shape[1]
    return pl.pallas_call(
        pack_kernel,
        out_shape=(shaped(rows, width),) * 3,
        in_specs=[VMEM] * 5,
        out_specs=(VMEM,) * 3,
        compiler_params=params(4),
        name="pack",
    )(one, two, three, piece, piece_across)


def gather_sums_kernel(cross, one, two, three, out):
    out[...] = (cross[...] + one[...]) + (two[...] + three[...])


def gather_sums(*parts):
    return pl.pallas_call(
        gather_sums_kernel,
        out_shape=shaped(*parts[0].shape),
        in_specs=[VMEM] * 4,
        out_specs=VMEM,
        compiler_params=params(3),
        cost_estimate=pl.CostEstimate(flops=SUMS_COST, bytes_accessed=0, transcendentals=0),
        name="gather_sums",
    )(*parts)


def unpack_kernel(where, home, one, two, three, piece, piece_across, back, weight_grad, bias_grad):
    back[...] = (home[...] + one[:TILE, :]) + (two[:TILE, :] + three[:TILE, :])
    rows = weight_grad.shape[0] // (X * YH)
    step = rows + 8
    for distance, source in enumerate((None, three, two, one)):
        x = lax.rem(where[3] + distance, X)
        for across in range(YH):
            if source is None:
                value = (piece, piece_across)[across][:rows, :]
            else:
                start = TILE + across * step
                value = source[start : start + rows, :]
            index = x * YH + lax.rem(where[4] + across, YH)
            weight_grad[pl.ds(pl.multiple_of(index * rows, rows), rows), :] = value
    bias_grad[...] = piece[rows : rows + 1, :]


def unpack(where, home, one, two, three, piece, piece_across, shape):
    return pl.pallas_call(
        unpack_kernel,
        out_shape=(shaped(*home.shape), shaped(*shape), shaped(1, shape[1])),
        in_specs=[SMEM] + [VMEM] * 6,
        out_specs=(VMEM,) * 3,
        compiler_params=params(5),
        cost_estimate=pl.CostEstimate(flops=UNPACK_COST, bytes_accessed=0, transcendentals=0),
        name="unpack",
    )(where, home, one, two, three, piece, piece_across)


def final_kernel(back, partner, weight, result):
    result[...] = dot3(split(back[...] + partner[...]), split(weight[...]), ((1,), (1,)))


def final(back, partner, weight):
    return pl.pallas_call(
        final_kernel,
        out_shape=shaped(TILE, weight.shape[0]),
        in_specs=[VMEM] * 3,
        out_specs=VMEM,
        compiler_params=params(3),
        name="final",
    )(back, partner, weight)


def body(node_features, weight, bias, tile_values, tile_coords, tile_count, cotangent):
    values = tile_values[0, 0]
    local_nodes, width = node_features.shape
    row_count = lax.axis_size("row")
    col_count = lax.axis_size("col")
    factor = 1.0 / math.sqrt(local_nodes * row_count * col_count)

    place, count = tile_coords[0, 0], tile_count.reshape(1)
    row, col = lax.axis_index("row"), lax.axis_index("col")
    where = jnp.stack(
        [
            lax.div(col, 2 * YL),
            lax.rem(lax.div(col, 2), YL),
            lax.rem(col, 2),
            lax.div(row, YH),
            lax.rem(row, YH),
        ]
    )

    partner = h_swap(node_features)
    near = halve(
        node_features,
        x_shift(node_features, -1),
        x_shift(node_features, 2),
        x_shift(node_features, 1),
    )
    far = (partner, x_shift(partner, -1), x_shift(partner, 2), x_shift(partner, 1))
    keep_far, send_far, keep_near, send_near = forward(place, count, where, values, near, far)
    other_far = lax.ppermute(send_far, "col", CORE_SWAP)
    other_far, send_near = lax.optimization_barrier((other_far, send_near))
    tiles = add_cores(keep_far, other_far)
    tiles += add_cores(keep_near, lax.ppermute(send_near, "col", CORE_SWAP))
    tiles = dict(zip([(d, y) for d in FAR + NEAR for y in range(YL)], tiles))
    cot_other = lax.ppermute(cotangent, "col", Y_SWAP)
    low, high = (ring_z([tiles[d, y] for d in range(Z)]) for y in range(YL))
    summed = last_sum(*low, *high)
    summed, cot_other = lax.optimization_barrier((summed, cot_other))
    summed_other = lax.ppermute(summed, "col", Y_SWAP)
    output, grads, extra = middle(
        where, summed, summed_other, weight, bias.reshape(1, width), cotangent, cot_other
    )

    six, two = z_shift(grads, 2), z_shift(grads, -2)
    seven, one = z_shift(grads, 1), z_shift(grads, -1)
    parts = lax.all_to_all(extra, "row", 0, 0)
    parts = lax.all_to_all(spread(parts, Z), "col", 0, 0, axis_index_groups=Z_GROUPS)
    three, five = z_shift(two, -1), z_shift(six, 1)
    low, high = halves(two, six)
    low, high = z_shift(low, 2), z_shift(high, -2)
    own = join(grads, one, two, three, low, high, five, six, seven)
    other = [lax.ppermute(part, "col", CORE_SWAP) for part in own]
    piece = total_of(parts, factor)
    piece = piece + lax.ppermute(piece, "col", CORE_SWAP)
    piece_across = h_swap(piece)
    home, *near, cross, one, two, three = backward(place, count, where, values, own, other)
    near = pack(*near, piece, piece_across)
    sums = gather_sums(cross, x_shift(one, 1), x_shift(two, 2), x_shift(three, -1))
    near = [x_shift(part, distance) for part, distance in zip(near, (1, 2, -1))]
    back, weight_grad, bias_grad = unpack(where, home, *near, piece, piece_across, weight.shape)
    input_grad = final(back, h_swap(sums), weight)
    return (output, input_grad, weight_grad, bias_grad.reshape(width))


def solution(mesh):
    in_specs = (
        P(("col", "row"), None),
        P(),
        P(),
        P("row", "col", None, None, None),
        P("row", "col", None, None),
        P("row", "col"),
        P(("row", "col"), None),
    )
    out_specs = (P(("row", "col"), None), P(("col", "row"), None), P(), P())
    return jax.shard_map(body, mesh=mesh, in_specs=in_specs, out_specs=out_specs, check_vma=False)
```

```python
import functools
import math

import jax
import jax.numpy as jnp
from jax import lax
from jax.experimental import pallas as pl
from jax.experimental.pallas import tpu as pltpu
from jax.sharding import PartitionSpec as P

Z, YL = 8, 2
X, YH = 4, 2
TILE = 128
PAIR = YL * TILE
FAR, NEAR = (3, 4, 5, 6), (7, 0, 1, 2)
JOIN_COST = 10**12
HALVES_COST = 10**12
ROWS_COST = 10**12
UNPACK_COST = 10**10
SUMS_COST = 10**10
JOIN_PARTS = 4


def col_pairs(move):
    pairs = []
    for z in range(Z):
        for y in range(YL):
            for core in range(2):
                a, b, c = move(z, y, core)
                pairs.append(((z * YL + y) * 2 + core, (a * YL + b) * 2 + c))
    return pairs


CORE_SWAP = col_pairs(lambda z, y, core: (z, y, 1 - core))
Y_SWAP = col_pairs(lambda z, y, core: (z, 1 - y, core))
Z_GROUPS = [[(z * YL + y) * 2 + core for z in range(Z)] for y in range(YL) for core in range(2)]


def z_shift(value, distance):
    def move(z, y, core):
        return (z + (2 * core - 1) * distance) % Z, y, core

    return lax.ppermute(value, "col", col_pairs(move))


def row_pairs(move):
    pairs = []
    for x in range(X):
        for h in range(YH):
            a, b = move(x, h)
            pairs.append((x * YH + h, (a % X) * YH + b))
    return pairs


def x_shift(value, distance):
    return lax.ppermute(value, "row", row_pairs(lambda x, h: (x + distance, h)))


def h_swap(value):
    return lax.ppermute(value, "row", row_pairs(lambda x, h: (x, 1 - h)))


SMEM = pl.BlockSpec(memory_space=pltpu.SMEM)
VMEM = pl.BlockSpec(memory_space=pltpu.VMEM)


def params(mib):
    return pltpu.CompilerParams(vmem_limit_bytes=mib * 1024 * 1024)


def shaped(*shape):
    return jax.ShapeDtypeStruct(shape, jnp.float32)


def split(value):
    high = value.astype(jnp.bfloat16)
    low = (value - high.astype(jnp.float32)).astype(jnp.bfloat16)
    return high, low


def dot3(left, right, contract):
    def one(a, b):
        return lax.dot_general(a, b, (contract, ((), ())), preferred_element_type=jnp.float32)

    return one(left[0], right[0]) + (one(left[0], right[1]) + one(left[1], right[0]))


def locate(tile, where):
    mine = lax.rem(tile, 2) == where[2]
    away = lax.div(tile, 2 * YL) - where[0]
    distance = lax.rem(jnp.where(lax.rem(tile, 2) == 0, -away, away) + Z, Z)
    return mine, distance, lax.rem(lax.div(tile, 2), YL)


def halve_kernel(*refs):
    count = len(refs) - 2
    for j in range(count):
        refs[count][j], refs[count + 1][j] = split(refs[j][...])


def halve(*blocks):
    shape = jax.ShapeDtypeStruct((len(blocks),) + blocks[0].shape, jnp.bfloat16)
    return pl.pallas_call(
        halve_kernel,
        out_shape=(shape, shape),
        in_specs=[VMEM] * len(blocks),
        out_specs=(VMEM,) * 2,
        compiler_params=params(3),
        cost_estimate=pl.CostEstimate(flops=ROWS_COST, bytes_accessed=0, transcendentals=0),
        name="halve",
    )(*blocks)


def row_index(tile, where):
    across = lax.rem(lax.rem(tile, YH) + where[4], YH)
    return across * X + lax.rem(lax.div(tile, YH) - where[3] + X, X)


def forward_kernel(
    place, count, where, values, near_high, near_low, a, b, c, d,
    keep_far, send_far, keep_near, send_near, high, low,
):
    for out in (keep_far, send_far, keep_near, send_near):
        out[...] = jnp.zeros_like(out)
    for j, part in enumerate((a, b, c, d)):
        high[j], low[j] = near_high[j], near_low[j]
        high[X + j], low[X + j] = split(part[...])
    for k in range(values.shape[0]):
        col = row_index(place[k, 1], where)
        mine, distance, y = locate(place[k, 0], where)
        live = k < count[0]
        product = dot3(split(values[k]), (high[col], low[col]), ((1,), (0,)))
        is_far = (distance >= FAR[0]) & (distance <= FAR[-1])
        far = jnp.where(is_far, distance - FAR[0], 0) * YL + y
        near = jnp.where(is_far, 0, lax.rem(distance + Z - NEAR[0], Z)) * YL + y
        keep_far[far] += jnp.where(live & mine & is_far, product, 0.0)
        send_far[far] += jnp.where(live & ~mine & is_far, product, 0.0)
        keep_near[near] += jnp.where(live & mine & ~is_far, product, 0.0)
        send_near[near] += jnp.where(live & ~mine & ~is_far, product, 0.0)


def forward(place, count, where, values, near, far):
    width = far[0].shape[-1]
    parts = pltpu.VMEM((X * YH, TILE, width), jnp.bfloat16)
    return pl.pallas_call(
        forward_kernel,
        out_shape=(shaped(len(FAR) * YL, TILE, width),) * 2
        + (shaped(len(NEAR) * YL, TILE, width),) * 2,
        in_specs=[SMEM, SMEM, SMEM] + [VMEM] * 7,
        out_specs=(VMEM,) * 4,
        scratch_shapes=[parts, parts],
        compiler_params=params(12),
        name="forward_tiles",
    )(place, count, where, values, *near, *far)


def add_cores_kernel(first, second, *outs):
    for tile, out in enumerate(outs):
        out[...] = first[tile] + second[tile]


def add_cores(first, second):
    tiles = first.shape[0]
    return pl.pallas_call(
        add_cores_kernel,
        out_shape=(shaped(*first.shape[1:]),) * tiles,
        in_specs=[VMEM] * 2,
        out_specs=(VMEM,) * tiles,
        compiler_params=params(10),
        name="add_cores",
    )(first, second)


def ring_z(blocks):
    up, down = blocks[4], blocks[5]
    for step in (3, 2, 1):
        up = blocks[step] + z_shift(up, 1)
    for step in (6, 7):
        down = blocks[step] + z_shift(down, -1)
    return blocks[0], z_shift(up, 1), z_shift(down, -1)


def last_sum_kernel(*refs):
    out = refs[-1]
    for y in range(YL):
        part = refs[3 * y][...] + refs[3 * y + 1][...] + refs[3 * y + 2][...]
        out[y * TILE : (y + 1) * TILE, :] = part


def last_sum(*parts):
    return pl.pallas_call(
        last_sum_kernel,
        out_shape=shaped(PAIR, parts[0].shape[1]),
        in_specs=[VMEM] * len(parts),
        out_specs=VMEM,
        compiler_params=params(4),
        name="last_sum",
    )(*parts)


def middle_kernel(where, mine, other, weight, bias, cot_own, cot_other, output, grad, extra, cots):
    y = where[1]
    cots[y] = cot_own[...]
    cots[1 - y] = cot_other[...]
    cot = cots[...].reshape(grad.shape)
    summed = split(mine[...] + other[...])
    pre = dot3(summed, split(weight[...]), ((1,), (0,))) + bias[...]
    sigma = jax.nn.sigmoid(pre)
    value = cot * (sigma * (1.0 + pre * (1.0 - sigma)))
    grad[...] = value
    cots[...] = (pre * sigma).reshape(cots.shape)
    output[...] = cots[y]
    sums = jnp.broadcast_to(jnp.sum(value, axis=0, keepdims=True), (8, value.shape[1]))
    product = dot3(summed, split(value), ((0,), (0,)))
    pieces = extra.shape[0]
    rows = product.shape[0] // pieces
    for j in range(pieces):
        extra[j, :rows, :] = product[j * rows : (j + 1) * rows, :]
        extra[j, rows:, :] = sums


def middle(where, mine, other, weight, bias, cot_own, cot_other):
    depth, width = weight.shape
    return pl.pallas_call(
        middle_kernel,
        out_shape=(
            shaped(TILE, width),
            shaped(PAIR, width),
            shaped(X * YH, depth // (X * YH) + 8, width),
        ),
        in_specs=[SMEM] + [VMEM] * 6,
        out_specs=(VMEM,) * 3,
        scratch_shapes=[pltpu.VMEM((YL, TILE, width), jnp.float32)],
        compiler_params=params(6),
        name="middle",
    )(where, mine, other, weight, bias, cot_own, cot_other)


def spread_kernel(parts, out):
    piece = parts[0]
    for j in range(1, parts.shape[0]):
        piece = piece + parts[j]
    for j in range(out.shape[0]):
        out[j] = piece


def spread(parts, copies):
    return pl.pallas_call(
        spread_kernel,
        out_shape=shaped(copies, *parts.shape[1:]),
        in_specs=[VMEM],
        out_specs=VMEM,
        compiler_params=params(4),
        name="spread",
    )(parts)


def halves_kernel(two, six, low, high):
    low[...] = six[:TILE, :]
    high[...] = two[TILE:, :]


def halves(two, six):
    return pl.pallas_call(
        halves_kernel,
        out_shape=(shaped(TILE, two.shape[1]),) * 2,
        in_specs=[VMEM] * 2,
        out_specs=(VMEM,) * 2,
        compiler_params=params(3),
        cost_estimate=pl.CostEstimate(flops=HALVES_COST, bytes_accessed=0, transcendentals=0),
        name="halves",
    )(two, six)


def join_kernel(*refs):
    parts, outs = refs[:-JOIN_PARTS], refs[-JOIN_PARTS:]
    rows, start = outs[0].shape[0], 0
    for part in parts:
        size = part.shape[0]
        outs[start // rows][start % rows : start % rows + size, :] = part[...]
        start += size


def join(*blocks):
    rows, width = sum(block.shape[0] for block in blocks), blocks[0].shape[1]
    return pl.pallas_call(
        join_kernel,
        out_shape=(shaped(rows // JOIN_PARTS, width),) * JOIN_PARTS,
        in_specs=[VMEM] * len(blocks),
        out_specs=(VMEM,) * JOIN_PARTS,
        compiler_params=params(8),
        cost_estimate=pl.CostEstimate(flops=JOIN_COST, bytes_accessed=0, transcendentals=0),
        name="join",
    )(*blocks)


def total_kernel(parts, out, *, factor):
    piece = parts[0]
    for j in range(1, parts.shape[0]):
        piece = piece + parts[j]
    out[...] = piece * factor


def total_of(parts, factor):
    return pl.pallas_call(
        functools.partial(total_kernel, factor=factor),
        out_shape=shaped(*parts.shape[1:]),
        in_specs=[VMEM],
        out_specs=VMEM,
        compiler_params=params(3),
        name="total",
    )(parts)


def backward_kernel(place, count, where, values, *refs):
    own, other = refs[:JOIN_PARTS], refs[JOIN_PARTS : 2 * JOIN_PARTS]
    outs, total = refs[2 * JOIN_PARTS : -1], refs[-1]
    total[...] = jnp.zeros_like(total)
    tiles = own[0].shape[0] // TILE
    for k in range(values.shape[0]):
        mine, distance, y = locate(place[k, 0], where)
        index = distance * YL + y
        rows = pl.ds(pl.multiple_of(lax.rem(index, tiles) * TILE, TILE), TILE)
        block = jnp.where(mine, own[0][rows, :], other[0][rows, :])
        for j in range(1, JOIN_PARTS):
            later = jnp.where(mine, own[j][rows, :], other[j][rows, :])
            block = jnp.where(index >= j * tiles, later, block)
        product = dot3(split(values[k]), split(block), ((0,), (0,)))
        total[row_index(place[k, 1], where)] += jnp.where(k < count[0], product, 0.0)
    for j, out in enumerate(outs):
        out[...] = total[j]


def backward(place, count, where, values, own, other):
    width = own[0].shape[1]
    return pl.pallas_call(
        backward_kernel,
        out_shape=(shaped(TILE, width),) * (X * YH),
        in_specs=[SMEM] * 3 + [VMEM] * (1 + 2 * JOIN_PARTS),
        out_specs=(VMEM,) * (X * YH),
        scratch_shapes=[pltpu.VMEM((X * YH, TILE, width), jnp.float32)],
        compiler_params=params(12),
        name="backward_tiles",
    )(place, count, where, values, *own, *other)


def pack_kernel(one, two, three, piece, piece_across, *outs):
    rows = piece.shape[0]
    for part, out in zip((one, two, three), outs):
        out[:TILE, :] = part[...]
        out[TILE : TILE + rows, :] = piece[...]
        out[TILE + rows :, :] = piece_across[...]


def pack(one, two, three, piece, piece_across):
    rows, width = one.shape[0] + 2 * piece.shape[0], one.shape[1]
    return pl.pallas_call(
        pack_kernel,
        out_shape=(shaped(rows, width),) * 3,
        in_specs=[VMEM] * 5,
        out_specs=(VMEM,) * 3,
        compiler_params=params(4),
        name="pack",
    )(one, two, three, piece, piece_across)


def gather_sums_kernel(cross, one, two, three, out):
    out[...] = (cross[...] + one[...]) + (two[...] + three[...])


def gather_sums(*parts):
    return pl.pallas_call(
        gather_sums_kernel,
        out_shape=shaped(*parts[0].shape),
        in_specs=[VMEM] * 4,
        out_specs=VMEM,
        compiler_params=params(3),
        cost_estimate=pl.CostEstimate(flops=SUMS_COST, bytes_accessed=0, transcendentals=0),
        name="gather_sums",
    )(*parts)


def near_sum_kernel(home, one, two, three, back):
    back[...] = (home[...] + one[:TILE, :]) + (two[:TILE, :] + three[:TILE, :])


def near_sum(home, one, two, three):
    return pl.pallas_call(
        near_sum_kernel,
        out_shape=shaped(*home.shape),
        in_specs=[VMEM] * 4,
        out_specs=VMEM,
        compiler_params=params(5),
        cost_estimate=pl.CostEstimate(flops=UNPACK_COST, bytes_accessed=0, transcendentals=0),
        name="near_sum",
    )(home, one, two, three)


def final_kernel(
    where, back, partner, weight, one, two, three, piece, piece_across, result, weight_grad, bias_grad
):
    result[...] = dot3(split(back[...] + partner[...]), split(weight[...]), ((1,), (1,)))
    rows = weight_grad.shape[0] // (X * YH)
    step = rows + 8
    for distance, source in enumerate((None, three, two, one)):
        x = lax.rem(where[3] + distance, X)
        for across in range(YH):
            if source is None:
                value = (piece, piece_across)[across][:rows, :]
            else:
                start = TILE + across * step
                value = source[start : start + rows, :]
            index = x * YH + lax.rem(where[4] + across, YH)
            weight_grad[pl.ds(pl.multiple_of(index * rows, rows), rows), :] = value
    bias_grad[...] = piece[rows : rows + 1, :]


def final(where, back, partner, weight, near, piece, piece_across):
    return pl.pallas_call(
        final_kernel,
        out_shape=(
            shaped(TILE, weight.shape[0]),
            shaped(*weight.shape),
            shaped(1, weight.shape[1]),
        ),
        in_specs=[SMEM] + [VMEM] * 8,
        out_specs=(VMEM,) * 3,
        compiler_params=params(6),
        name="final",
    )(where, back, partner, weight, *near, piece, piece_across)


def body(node_features, weight, bias, tile_values, tile_coords, tile_count, cotangent):
    values = tile_values[0, 0]
    local_nodes, width = node_features.shape
    row_count = lax.axis_size("row")
    col_count = lax.axis_size("col")
    factor = 1.0 / math.sqrt(local_nodes * row_count * col_count)

    place, count = tile_coords[0, 0], tile_count.reshape(1)
    row, col = lax.axis_index("row"), lax.axis_index("col")
    where = jnp.stack(
        [
            lax.div(col, 2 * YL),
            lax.rem(lax.div(col, 2), YL),
            lax.rem(col, 2),
            lax.div(row, YH),
            lax.rem(row, YH),
        ]
    )

    partner = h_swap(node_features)
    near = halve(
        node_features,
        x_shift(node_features, -1),
        x_shift(node_features, 2),
        x_shift(node_features, 1),
    )
    far = (partner, x_shift(partner, -1), x_shift(partner, 2), x_shift(partner, 1))
    keep_far, send_far, keep_near, send_near = forward(place, count, where, values, near, far)
    other_far = lax.ppermute(send_far, "col", CORE_SWAP)
    other_far, send_near = lax.optimization_barrier((other_far, send_near))
    tiles = add_cores(keep_far, other_far)
    tiles += add_cores(keep_near, lax.ppermute(send_near, "col", CORE_SWAP))
    tiles = dict(zip([(d, y) for d in FAR + NEAR for y in range(YL)], tiles))
    cot_other = lax.ppermute(cotangent, "col", Y_SWAP)
    low, high = (ring_z([tiles[d, y] for d in range(Z)]) for y in range(YL))
    summed = last_sum(*low, *high)
    summed, cot_other = lax.optimization_barrier((summed, cot_other))
    summed_other = lax.ppermute(summed, "col", Y_SWAP)
    output, grads, extra = middle(
        where, summed, summed_other, weight, bias.reshape(1, width), cotangent, cot_other
    )

    six, two = z_shift(grads, 2), z_shift(grads, -2)
    seven, one = z_shift(grads, 1), z_shift(grads, -1)
    parts = lax.all_to_all(extra, "row", 0, 0)
    parts = lax.all_to_all(spread(parts, Z), "col", 0, 0, axis_index_groups=Z_GROUPS)
    three, five = z_shift(two, -1), z_shift(six, 1)
    low, high = halves(two, six)
    low, high = z_shift(low, 2), z_shift(high, -2)
    own = join(grads, one, two, three, low, high, five, six, seven)
    other = [lax.ppermute(part, "col", CORE_SWAP) for part in own]
    piece = total_of(parts, factor)
    piece = piece + lax.ppermute(piece, "col", CORE_SWAP)
    piece_across = h_swap(piece)
    home, *near, cross, one, two, three = backward(place, count, where, values, own, other)
    near = pack(*near, piece, piece_across)
    sums = gather_sums(cross, x_shift(one, 1), x_shift(two, 2), x_shift(three, -1))
    near = [x_shift(part, distance) for part, distance in zip(near, (1, 2, -1))]
    back = near_sum(home, *near)
    input_grad, weight_grad, bias_grad = final(
        where, back, h_swap(sums), weight, near, piece, piece_across
    )
    return (output, input_grad, weight_grad, bias_grad.reshape(width))


def solution(mesh):
    in_specs = (
        P(("col", "row"), None),
        P(),
        P(),
        P("row", "col", None, None, None),
        P("row", "col", None, None),
        P("row", "col"),
        P(("row", "col"), None),
    )
    out_specs = (P(("row", "col"), None), P(("col", "row"), None), P(), P())
    return jax.shard_map(body, mesh=mesh, in_specs=in_specs, out_specs=out_specs, check_vma=False)
```
